32 devices in a mesh: gx: 16 (over z, y, x), gy: 2 (over core).
Axes of the slice: x: 2, y: 2, z: 4, core: 2. Of those that a mesh axis runs over, the one named last changes fastest.
Arguments:
- motion: float32 [3, 32, 96, 256], P(None, 'gx', None, 'gy'), may hold values from -6 to 6
- stress: float32 [6, 32, 96, 256], P(None, 'gx', None, 'gy'), may hold values from -6 to 6
- buoyancy: float32 [32, 96, 256], P('gx', None, 'gy'), may hold values from 0.5 to 1.5
- lame_first: float32 [32, 96, 256], P('gx', None, 'gy'), may hold values from 0.5 to 1.5
- lame_shear: float32 [32, 96, 256], P('gx', None, 'gy'), may hold values from 0.5 to 1.5
- surface: float32 [256, 2048], P('gx', 'gy'), may hold values from -2 to 2
- momentum: float32 [2, 256, 2048], P(None, 'gx', 'gy'), may hold values from -3 to 3
- bathymetry: float32 [256, 2048], P('gx', 'gy'), may hold values from 2 to 4
- wet_mask: int32 [256, 2048], P('gx', 'gy'), may hold values 0 or 1
Outputs:
- final_motion: float32 [3, 32, 96, 256], P(None, 'gx', None, 'gy')
- final_stress: float32 [6, 32, 96, 256], P(None, 'gx', None, 'gy')
- final_surface: float32 [256, 2048], P('gx', 'gy')
- final_momentum: float32 [2, 256, 2048], P(None, 'gx', 'gy')
The draws below stay inside these ranges and needn't reach their ends.
Inputs may be any that keep to these rules, and one draw needn't show every extreme that they name: `wet_mask`: 1 marks a wet ocean cell, 0 a dry one.
All inputs are finite; a program needn't handle non-finite values. No bound on the sum of `wet_mask` on one device may be relied on, other than what follows from the above.
Results may differ from the reference program's by a relative error of at most 0.0001.
Values sent between devices are 32-bit elements; how exact they have to be, the bound alone decides.
A program may use at most 64 MiB of HBM per device.

```python
import jax
import jax.numpy as jnp

SX = 2
Z = 96
RATIO = 8
STEPS = 4
NSUB = 4
NXS = 32
NYS = 256
NXO = 256
NYO = 2048


def touch_ends(result, key, least, high):
    extent = result.shape
    place = [jax.random.randint(jax.random.fold_in(key, axis), (), 0, extent[axis]) for axis in range(len(extent))]
    result = result.at[tuple(place)].set(least)
    longest = extent.index(max(extent))
    place[longest] = (place[longest] + 1) % extent[longest]
    return result.at[tuple(place)].set(high)


def steps_of(own_key, dims, cuts, least, high):
    level, own = 1.0, jax.random.fold_in(own_key, 6)
    for axis_at, blocks in cuts:
        heights = jnp.exp(jax.random.uniform(jax.random.fold_in(own, axis_at), (blocks,), jnp.float32, least / len(cuts), high / len(cuts)))
        level = level * jnp.repeat(heights, dims[axis_at] // blocks).reshape([-1 if axis == axis_at else 1 for axis in range(len(dims))])
    return level


def gaussian(stream_key, extent, width, most, shards=(), held_as=jnp.bfloat16):
    result = width * jax.random.normal(stream_key, extent, jnp.float32)
    if shards:
        result = result * steps_of(stream_key, extent, shards, -0.22, 0.18)
    return jnp.clip(result, -most, most).astype(held_as)


def setup_inputs(seed: int = 0) -> dict:
    seeds = jax.random.split(jax.random.key(seed), 10)
    return {
        "motion": gaussian(seeds[0], (3, NXS, Z, NYS), 1.0, 6.0, ((1, 16), (3, 2)), jnp.float32),
        "stress": gaussian(seeds[1], (6, NXS, Z, NYS), 1.0, 6.0, ((1, 16), (3, 2)), jnp.float32),
        "buoyancy": jnp.clip(0.5 + 1.0 * jax.random.uniform(seeds[2], (NXS, Z, NYS), jnp.float32) ** steps_of(seeds[2], (NXS, Z, NYS), ((0, 16), (2, 2)), -0.2, 0.2), 0.5, 1.5),
        "lame_first": jnp.clip(0.5 + 1.0 * jax.random.uniform(seeds[3], (NXS, Z, NYS), jnp.float32) ** steps_of(seeds[3], (NXS, Z, NYS), ((0, 16), (2, 2)), -0.2, 0.2), 0.5, 1.5),
        "lame_shear": jnp.clip(0.5 + 1.0 * jax.random.uniform(seeds[4], (NXS, Z, NYS), jnp.float32) ** steps_of(seeds[4], (NXS, Z, NYS), ((0, 16), (2, 2)), -0.2, 0.2), 0.5, 1.5),
        "surface": gaussian(seeds[5], (NXO, NYO), 0.25, 2.0, ((0, 16), (1, 2)), jnp.float32),
        "momentum": gaussian(seeds[6], (2, NXO, NYO), 0.5, 3.0, ((1, 16), (2, 2)), jnp.float32),
        "bathymetry": jnp.clip(2.0 + 2.0 * jax.random.uniform(seeds[7], (NXO, NYO), jnp.float32) ** steps_of(seeds[7], (NXO, NYO), ((0, 16), (1, 2)), -0.2, 0.2), 2.0, 4.0),
        "wet_mask": touch_ends((jax.random.randint(seeds[8], (NXO, NYO), 0, 8) < 7).astype(jnp.int32), jax.random.fold_in(seeds[8], 1), 0, 1),
    }


SOLID_STEP = 0.2
WAVE_STEP = 0.1
VISCOSITY = 0.05
UPLIFT_GAIN = 0.25
LOAD_GAIN = 8.0


def middle(quantity):
    return quantity[1:-1, :, 1:-1]


def ahead_x(quantity):
    return quantity[2:, :, 1:-1]


def behind_x(quantity):
    return quantity[:-2, :, 1:-1]


def ahead_y(quantity):
    return quantity[1:-1, :, 2:]


def behind_y(quantity):
    return quantity[1:-1, :, :-2]


def ahead_z(quantity):
    return jnp.concatenate([quantity[:, 1:], jnp.zeros_like(quantity[:, :1])], axis=1)


def behind_z(quantity):
    return jnp.concatenate([jnp.zeros_like(quantity[:, :1]), quantity[:, :-1]], axis=1)


def advance_velocity(motion, stress, buoyancy):
    stress_xx, stress_yy, stress_zz = stress[0], stress[1], stress[2]
    stress_xy, stress_xz, stress_yz = stress[3], stress[4], stress[5]
    mid_xy = middle(stress_xy)
    mid_xz = middle(stress_xz)
    mid_yz = middle(stress_yz)
    mid_zz = middle(stress_zz)
    step_rate = SOLID_STEP * buoyancy
    force_x = (ahead_x(stress_xx) - middle(stress_xx)) + (mid_xy - behind_y(stress_xy)) + (mid_xz - behind_z(mid_xz))
    force_y = (mid_xy - behind_x(stress_xy)) + (ahead_y(stress_yy) - middle(stress_yy)) + (mid_yz - behind_z(mid_yz))
    force_z = (mid_xz - behind_x(stress_xz)) + (mid_yz - behind_y(stress_yz)) + (ahead_z(mid_zz) - mid_zz)
    return jnp.stack([motion[0] + step_rate * force_x, motion[1] + step_rate * force_y, motion[2] + step_rate * force_z])


def advance_stress(stress, motion, lame_first, lame_shear):
    speed_x, speed_y, speed_z = motion[0], motion[1], motion[2]
    centre_x = middle(speed_x)
    centre_y = middle(speed_y)
    centre_z = middle(speed_z)
    strain_x = centre_x - behind_x(speed_x)
    strain_y = centre_y - behind_y(speed_y)
    strain_z = centre_z - behind_z(centre_z)
    stiffness = lame_first + 2.0 * lame_shear
    normal_xx = stress[0] + SOLID_STEP * (stiffness * strain_x + lame_first * (strain_y + strain_z))
    normal_yy = stress[1] + SOLID_STEP * (stiffness * strain_y + lame_first * (strain_x + strain_z))
    normal_zz = stress[2] + SOLID_STEP * (stiffness * strain_z + lame_first * (strain_x + strain_y))
    shear_rate = SOLID_STEP * lame_shear
    shear_xy = stress[3] + shear_rate * ((ahead_y(speed_x) - centre_x) + (ahead_x(speed_y) - centre_y))
    shear_xz = stress[4] + shear_rate * ((ahead_z(centre_x) - centre_x) + (ahead_x(speed_z) - centre_z))
    shear_yz = stress[5] + shear_rate * ((ahead_z(centre_y) - centre_y) + (ahead_y(speed_z) - centre_z))
    return jnp.stack([normal_xx, normal_yy, normal_zz, shear_xy, shear_xz, shear_yz])


def apply_load(stress, seafloor_load):
    return stress.at[2, :, 0, :].set(-LOAD_GAIN * seafloor_load)


def interior(quantity):
    return quantity[1:-1, 1:-1]


def wave_substep(ocean_state, seabed):
    height, flow_x, flow_y = ocean_state[0], ocean_state[1], ocean_state[2]
    depth_in = seabed[0, 1:-1, 1:-1]
    wet_full = seabed[1]
    wet_in = wet_full[1:-1, 1:-1]
    extent_x, extent_y = height.shape
    height_new = height[1:, 1:] - WAVE_STEP * wet_in[1:, 1:] * ((flow_x[1:, 1:] - flow_x[:-1, 1:]) + (flow_y[1:, 1:] - flow_y[1:, :-1]))
    centre = height_new[:-1, :-1]
    east_side = height_new[1:, :-1]
    north_side = height_new[:-1, 1:]
    face_x = wet_full[:-1, :] * wet_full[1:, :]
    face_y = wet_full[:, :-1] * wet_full[:, 1:]
    flow_cx = interior(flow_x)
    spread_x = (face_x[3:extent_x + 1, 2:extent_y] * (flow_x[2:, 1:-1] - flow_cx)
                + face_x[1:extent_x - 1, 2:extent_y] * (flow_x[:-2, 1:-1] - flow_cx)
                + face_x[2:extent_x, 3:extent_y + 1] * (flow_x[1:-1, 2:] - flow_cx)
                + face_x[2:extent_x, 1:extent_y - 1] * (flow_x[1:-1, :-2] - flow_cx))
    flow_cy = interior(flow_y)
    spread_y = (face_y[3:extent_x + 1, 2:extent_y] * (flow_y[2:, 1:-1] - flow_cy)
                + face_y[1:extent_x - 1, 2:extent_y] * (flow_y[:-2, 1:-1] - flow_cy)
                + face_y[2:extent_x, 3:extent_y + 1] * (flow_y[1:-1, 2:] - flow_cy)
                + face_y[2:extent_x, 1:extent_y - 1] * (flow_y[1:-1, :-2] - flow_cy))
    depth_c = interior(depth_in)
    depth_east = depth_in[2:, 1:-1]
    depth_north = depth_in[1:-1, 2:]
    new_flow_x = face_x[2:extent_x, 2:extent_y] * (flow_cx - WAVE_STEP * 0.5 * (depth_c + depth_east + centre + east_side) * (east_side - centre) + VISCOSITY * spread_x)
    new_flow_y = face_y[2:extent_x, 2:extent_y] * (flow_cy - WAVE_STEP * 0.5 * (depth_c + depth_north + centre + north_side) * (north_side - centre) + VISCOSITY * spread_y)
    return jnp.stack([centre, new_flow_x, new_flow_y])


def upsample(coarse):
    count_x, count_y = coarse.shape
    spread_out = jnp.broadcast_to(coarse[:, None, :, None], (count_x, RATIO, count_y, RATIO))
    return spread_out.reshape(count_x * RATIO, count_y * RATIO)


def block_average(fine_grid):
    count_x, count_y = fine_grid.shape
    return jnp.mean(fine_grid.reshape(count_x // RATIO, RATIO, count_y // RATIO, RATIO), axis=(1, 3))


def reference(motion, stress, buoyancy, lame_first, lame_shear, surface, momentum, bathymetry, wet_mask):
    wet_float = wet_mask.astype(jnp.float32)
    seabed = jnp.pad(jnp.stack([bathymetry, wet_float]), ((0, 0), (2, 2), (2, 2)))
    ocean_state = jnp.concatenate([surface[None], momentum], axis=0)
    half_rows = SX // 2
    count_x = motion.shape[1]
    count_y = motion.shape[3]
    zero_rows = jnp.zeros((half_rows, count_y), jnp.float32)
    for coupling_step in range(STEPS):
        top_speed = motion[2, :, 0, :]
        uplift = jnp.concatenate([zero_rows, top_speed[:count_x - half_rows]], axis=0)
        lifted = ocean_state[0] + UPLIFT_GAIN * wet_float * upsample(uplift)
        ocean_state = ocean_state.at[0].set(lifted)
        for substep in range(NSUB):
            padded = jnp.pad(ocean_state, ((0, 0), (1, 1), (1, 1)))
            ocean_state = wave_substep(padded, seabed)
        averaged = block_average(wet_float * ocean_state[0])
        seafloor_load = jnp.concatenate([averaged[half_rows:], zero_rows], axis=0)
        stress_padded = jnp.pad(stress, ((0, 0), (1, 1), (0, 0), (1, 1)))
        motion = advance_velocity(motion, stress_padded, buoyancy)
        motion_padded = jnp.pad(motion, ((0, 0), (1, 1), (0, 0), (1, 1)))
        stress = advance_stress(stress, motion_padded, lame_first, lame_shear)
        stress = apply_load(stress, seafloor_load)
    return motion, stress, ocean_state[0], ocean_state[1:]
```

```python
import functools

import jax
import jax.numpy as jnp
from jax import lax
from jax.experimental import pallas as pl
from jax.experimental.pallas import tpu as pltpu
from jax.sharding import PartitionSpec as P

RATIO = 8
STEPS = 4
NSUB = 4
SOLID_STEP = 0.2
WAVE_STEP = 0.1
VISCOSITY = 0.05
UPLIFT_GAIN = 0.25
LOAD_GAIN = 8.0

MESH = pl.DeviceIdType.MESH
F32 = jnp.float32


def kernel(
    nx, ny,
    motion, stress, buoy, lame1, lame2, surf, mom, bath, wetm,
    o_motion, o_stress, o_surf, o_mom,
    S, V, Bu, L1, L2, H, M, N, Wi, W, D, wt, Dx, Dy, Ax, Bx, Ay, By, Fx, Up,
    hb_s, ha_xx, hd_xy, hd_yz, hu_yy,
    hb_vx, ha_v, hd_vy, hu_vx, hu_vz,
    cu, cd, hd_c, hu_c,
    xf, xb, hb_x, ha_x, xsf, xsb, hb_xs, ha_xs,
    ls, lr, tops,
    in_sem, send, recv, csend, crecv, xsend, xrecv, lsend, lrecv,
):
    gx = lax.axis_index("gx")
    gy = lax.axis_index("gy")
    has_b, has_a, has_d, has_u = gx > 0, gx < nx - 1, gy > 0, gy < ny - 1
    ahead = (jnp.minimum(gx + 1, nx - 1), gy)
    behind = (jnp.maximum(gx - 1, 0), gy)
    up = (gx, jnp.minimum(gy + 1, ny - 1))
    down = (gx, jnp.maximum(gy - 1, 0))
    dirs = {
        "f": (ahead, has_a, has_b),
        "b": (behind, has_b, has_a),
        "u": (up, has_u, has_d),
        "d": (down, has_d, has_u),
    }
    zdim = S.shape[2]
    lanes = H.shape[1]
    own = surf.shape[1]
    nt = lanes // 128

    loads = [
        pltpu.make_async_copy(a, b, in_sem.at[i])
        for i, (a, b) in enumerate([
            (wetm, Wi),
            (bath, D.at[pl.ds(0, 16), pl.ds(0, own)]),
            (surf, H.at[pl.ds(0, 16), pl.ds(0, own)]),
            (mom.at[0], M.at[pl.ds(0, 16), pl.ds(0, own)]),
            (mom.at[1], N.at[pl.ds(0, 16), pl.ds(0, own)]),
            (motion, V), (stress, S), (buoy, Bu), (lame1, L1), (lame2, L2),
        ])
    ]
    for c in loads:
        c.start()

    def zero_when_absent(flag, refs):
        @pl.when(jnp.logical_not(flag))
        def _():
            for r in refs:
                r[...] = jnp.zeros(r.shape, F32)

    zero_when_absent(has_b, [hb_s, hb_vx, hb_x, hb_xs])
    zero_when_absent(has_a, [ha_xx, ha_v, ha_x, ha_xs, lr])
    zero_when_absent(has_d, [hd_xy, hd_yz, hd_vy, hd_c])
    zero_when_absent(has_u, [hu_yy, hu_vx, hu_vz, hu_c])
    for r in (cu, cd, xf, xb, xsf, xsb, ls, tops):
        r[...] = jnp.zeros(r.shape, F32)

    barrier = pltpu.get_barrier_semaphore()
    for d in "fbud":
        dev, ok, _ = dirs[d]

        @pl.when(ok)
        def _():
            pl.semaphore_signal(barrier, inc=1, device_id=dev, device_id_type=MESH)

    pl.semaphore_wait(barrier, sum(f.astype(jnp.int32) for f in (has_b, has_a, has_d, has_u)))

    class Msg:
        def __init__(self, d, src, dst, ssem, rsem):
            dev, self.ok, self.inc = dirs[d]
            self.c = pltpu.make_async_remote_copy(
                src_ref=src, dst_ref=dst, send_sem=ssem, recv_sem=rsem,
                device_id=dev, device_id_type=MESH)

        def start(self):
            pl.when(self.ok)(lambda: self.c.start())

        def sent(self):
            pl.when(self.ok)(lambda: self.c.wait_send())

        def got(self):
            pl.when(self.inc)(lambda: self.c.wait_recv())

    count = [0]

    def msg(d, src, dst):
        i = count[0]
        count[0] += 1
        return Msg(d, src, dst, send.at[i], recv.at[i])

    am = [
        msg("f", S.at[pl.ds(3, 2), 1], hb_s),
        msg("b", S.at[0, 0], ha_xx),
        msg("u", S.at[3], hd_xy),
        msg("u", S.at[5], hd_yz),
        msg("d", S.at[1], hu_yy),
    ]
    bm = [
        msg("f", V.at[0, 1], hb_vx),
        msg("b", V.at[pl.ds(1, 2), 0], ha_v),
        msg("u", V.at[1], hd_vy),
        msg("d", V.at[0], hu_vx),
        msg("d", V.at[2], hu_vz),
    ]
    xsm = [msg("f", xsf, hb_xs), msg("b", xsb, ha_xs)]

    def xm(slot):
        return [
            Msg("f", xf.at[slot], hb_x.at[slot], xsend.at[0, slot], xrecv.at[0, slot]),
            Msg("b", xb.at[slot], ha_x.at[slot], xsend.at[1, slot], xrecv.at[1, slot]),
        ]

    def cm(slot):
        return [
            Msg("u", cu.at[slot], hd_c.at[slot], csend.at[0, slot], crecv.at[0, slot]),
            Msg("d", cd.at[slot], hu_c.at[slot], csend.at[1, slot], crecv.at[1, slot]),
        ]

    def lm(slot):
        return Msg("b", ls.at[slot], lr.at[slot], lsend.at[slot], lrecv.at[slot])

    lane = lax.broadcasted_iota(jnp.int32, (zdim, 128), 1)
    zrow = lax.broadcasted_iota(jnp.int32, (zdim, 128), 0)
    lane16 = lax.broadcasted_iota(jnp.int32, (16, 128), 1)
    lane8 = lax.broadcasted_iota(jnp.int32, (8, 128), 1)

    def ym(p, halo):
        return pltpu.roll(jnp.where(lane == 127, halo, p), 1, 1)

    def yp(p, halo):
        return pltpu.roll(jnp.where(lane == 0, halo, p), 127, 1)

    def zm(p):
        return jnp.where(zrow == 0, 0.0, pltpu.roll(p, 1, 0))

    def zp(p):
        return jnp.where(zrow == zdim - 1, 0.0, pltpu.roll(p, zdim - 1, 0))

    def rm(a):
        return pltpu.roll(a, 1, 0)

    def rp(a):
        return pltpu.roll(a, a.shape[0] - 1, 0)

    def cmn(a):
        return pltpu.roll(a, 1, 1)

    def cpl(a):
        return pltpu.roll(a, a.shape[1] - 1, 1)

    def fill_c(slot):
        for i, r in enumerate((H, M, N)):
            cu[slot, 16 * i:16 * i + 16, :] = r[0:16, own - 128:own]
            cd[slot, 16 * i:16 * i + 16, :] = r[0:16, 0:128]
        t = jnp.concatenate([V[2, 0, 0:1, :], V[2, 1, 0:1, :]], axis=0)
        cu[slot, 48:50, :] = t
        cd[slot, 48:50, :] = t
        tops[1:3, 0:128] = t

    def use_c(slot):
        for i, r in enumerate((H, M, N)):
            r[0:16, own:lanes] = jnp.where(
                lane16 < 64, hu_c[slot, 16 * i:16 * i + 16, :], hd_c[slot, 16 * i:16 * i + 16, :])
        t = jnp.where(lane8 < 8, hu_c[slot, 48:56, :], pltpu.roll(hd_c[slot, 48:56, :], 16, 1))
        tops[1:3, 128:256] = t[0:2, :]

    def fill_x(slot):
        for i, r in enumerate((H, M, N)):
            xf[slot, 4 * i:4 * i + 4, :] = r[12:16, :]
            xb[slot, 4 * i:4 * i + 4, :] = r[0:4, :]
        xf[slot, 12:14, 0:256] = tops[1:3, :]

    def start_all(ms):
        for m in ms:
            m.start()

    for c in loads[:6]:
        c.wait()
    W[0:16, 0:own] = Wi[...].astype(F32)
    for i, r in enumerate((W, D)):
        cu[0, 56 + 16 * i:72 + 16 * i, :] = r[0:16, own - 128:own]
        cd[0, 56 + 16 * i:72 + 16 * i, :] = r[0:16, 0:128]
    fill_c(0)
    start_all(cm(0))
    loads[6].wait()
    start_all(am)
    for c in loads[7:]:
        c.wait()
    for m in cm(0):
        m.got()
    use_c(0)
    for i, r in enumerate((W, D)):
        r[0:16, own:lanes] = jnp.where(
            lane16 < 64, hu_c[0, 56 + 16 * i:72 + 16 * i, :], hd_c[0, 56 + 16 * i:72 + 16 * i, :])
    for i, r in enumerate((W, D)):
        xsf[4 * i:4 * i + 4, :] = r[12:16, :]
        xsb[4 * i:4 * i + 4, :] = r[0:4, :]
    xsb[8:12, :] = W[0:4, :] * W[1:5, :]
    fill_x(0)
    start_all(xsm)
    start_all(xm(0))

    def ocean_setup():
        for m in xsm:
            m.got()
        for i, r in enumerate((W, D)):
            r[16:24, :] = jnp.concatenate(
                [ha_xs[4 * i:4 * i + 4, :], hb_xs[4 * i:4 * i + 4, :]], axis=0)
        w = W[...]
        d = D[...]
        fx = w * rp(w)
        Fx[...] = fx
        Fx[16:20, :] = ha_xs[8:12, :]
        fx = Fx[...]
        fy = w * cpl(w)
        wt[...] = WAVE_STEP * w
        Dx[...] = d + rp(d)
        Dy[...] = d + cpl(d)
        Bx[...] = VISCOSITY * fx
        By[...] = VISCOSITY * fy
        Ax[...] = fx * (1.0 - VISCOSITY * (rp(fx) + rm(fx) + cpl(fx) + cmn(fx)))
        Ay[...] = fy * (1.0 - VISCOSITY * (rp(fy) + rm(fy) + cpl(fy) + cmn(fy)))

    def mask_flow():
        fx = Fx[...]
        fy = W[...] * cpl(W[...])
        m, n = M[...], N[...]
        mm, nn = fx * m, fy * n
        dm, dn = m - mm, n - nn
        H[...] = H[...] - wt[...] * ((dm - rm(dm)) + (dn - cmn(dn)))
        M[...] = mm
        N[...] = nn

    def substep(_, carry):
        m, n = M[...], N[...]
        mw, ns = rm(m), cmn(n)
        h = H[...] - wt[...] * ((m - mw) + (n - ns))
        H[...] = h
        he, hn = rp(h), cpl(h)
        M[...] = Ax[...] * m + Bx[...] * (
            ((rp(m) + mw) + (cpl(m) + cmn(m))) - (Dx[...] + h + he) * (he - h))
        N[...] = Ay[...] * n + By[...] * (
            ((rp(n) + rm(n)) + (cpl(n) + ns)) - (Dy[...] + h + hn) * (hn - h))
        return carry

    er = lax.broadcasted_iota(jnp.int32, (128, 128), 0)
    ec = lax.broadcasted_iota(jnp.int32, (128, 128), 1)
    row24 = lax.broadcasted_iota(jnp.int32, (24, 128), 0)

    def lift(slot):
        b = hb_x[slot, 12:14, 0:256]
        tops[0:1, :] = b[1:2, :]
        tops[3:4, :] = b[0:1, :]
        t = tops[:, 0:128]
        tiles = [t] + [pltpu.roll(t, 128 - 16 * q, 1) for q in range(1, nt - 1)]
        tiles.append(tops[:, 128:256])
        spread = jnp.where((ec // RATIO) == er, 1.0, 0.0)
        u = jnp.dot(jnp.concatenate(tiles, axis=0), spread,
                    preferred_element_type=F32, precision=lax.Precision.HIGHEST)
        for q in range(nt):
            r = u[8 * q:8 * q + 8, :]
            e = [jnp.broadcast_to(r[i:i + 1, :], (24, 128)) for i in range(4)]
            full = jnp.where(row24 < 8, e[0], jnp.where(row24 < 16, e[1], jnp.where(row24 < 20, e[2], e[3])))
            at = slice(128 * q, 128 * q + 128)
            Up[:, at] = full
        H[...] = H[...] + UPLIFT_GAIN * W[...] * Up[...]

    def average(slot):
        p = W[0:16, 0:own] * H[0:16, 0:own]
        parts = [p[:, 128 * q:128 * q + 128] for q in range(nt - 1)]
        gather = jnp.where((er // RATIO) == ec, 1.0, 0.0)
        g = jnp.dot(jnp.concatenate(parts, axis=0), gather,
                    preferred_element_type=F32, precision=lax.Precision.HIGHEST)
        a0 = jnp.zeros((1, 128), F32)
        a1 = jnp.zeros((1, 128), F32)
        for q in range(nt - 1):
            s0 = jnp.sum(g[16 * q:16 * q + 8, :], axis=0, keepdims=True)
            s1 = jnp.sum(g[16 * q + 8:16 * q + 16, :], axis=0, keepdims=True)
            two = jnp.concatenate([s0, s1, jnp.zeros((6, 128), F32)], axis=0)
            if q:
                two = pltpu.roll(two, 16 * q, 1)
            a0 = a0 + two[0:1, :]
            a1 = a1 + two[1:2, :]
        scale = -LOAD_GAIN / (RATIO * RATIO)
        ls[slot, 0:1, :] = a0 * scale
        ls[slot, 1:2, :] = a1 * scale

    def apply_load(slot):
        lm(slot).got()
        S[2, 0, 0:1, :] = ls[slot, 1:2, :]
        S[2, 1, 0:1, :] = lr[slot, 0:1, :]

    def step(k, carry):
        slot = lax.rem(k, 2)
        nslot = lax.rem(k + 1, 2)
        for m in am:
            m.got()

        @pl.when(k > 0)
        def _():
            apply_load(nslot)

        for x in range(2):
            sb = SOLID_STEP * Bu[x]
            xx, yy, zz, xy, xz, yz = (S[c, x] for c in range(6))
            xx_a = S[0, 1] if x == 0 else ha_xx[...]
            xy_b = hb_s[0] if x == 0 else S[3, 0]
            xz_b = hb_s[1] if x == 0 else S[4, 0]
            V[0, x] = V[0, x] + sb * ((xx_a - xx) + (xy - ym(xy, hd_xy[x])) + (xz - zm(xz)))
            V[1, x] = V[1, x] + sb * ((xy - xy_b) + (yp(yy, hu_yy[x]) - yy) + (yz - zm(yz)))
            V[2, x] = V[2, x] + sb * ((xz - xz_b) + (yz - ym(yz, hd_yz[x])) + (zp(zz) - zz))
        start_all(bm)

        xms = xm(slot)
        for m in xms:
            m.got()
        for i, r in enumerate((H, M, N)):
            r[16:24, :] = jnp.concatenate(
                [ha_x[slot, 4 * i:4 * i + 4, :], hb_x[slot, 4 * i:4 * i + 4, :]], axis=0)

        @pl.when(k == 0)
        def _():
            ocean_setup()
            mask_flow()

        lift(slot)
        lax.fori_loop(0, NSUB, substep, 0)
        average(slot)
        lm(slot).start()

        for m in cm(slot):
            m.sent()

        @pl.when(k < STEPS - 1)
        def _():
            fill_c(nslot)
            start_all(cm(nslot))

        for m in am:
            m.sent()
        for m in bm:
            m.got()
        for x in range(2):
            vx, vy, vz = V[0, x], V[1, x], V[2, x]
            vx_b = hb_vx[...] if x == 0 else V[0, 0]
            vy_a = V[1, 1] if x == 0 else ha_v[0]
            vz_a = V[2, 1] if x == 0 else ha_v[1]
            ex = vx - vx_b
            ey = vy - ym(vy, hd_vy[x])
            ez = vz - zm(vz)
            l, g = SOLID_STEP * L1[x], SOLID_STEP * L2[x]
            tr = l * (ex + ey + ez)
            g2 = 2.0 * g
            S[0, x] = S[0, x] + (tr + g2 * ex)
            S[1, x] = S[1, x] + (tr + g2 * ey)
            S[2, x] = S[2, x] + (tr + g2 * ez)
            S[3, x] = S[3, x] + g * ((yp(vx, hu_vx[x]) - vx) + (vy_a - vy))
            S[4, x] = S[4, x] + g * ((zp(vx) - vx) + (vz_a - vz))
            S[5, x] = S[5, x] + g * ((zp(vy) - vy) + (yp(vz, hu_vz[x]) - vz))

        @pl.when(k < STEPS - 1)
        def _():
            start_all(am)
            for m in cm(nslot):
                m.got()
            use_c(nslot)
            fill_x(nslot)
            start_all(xm(nslot))

        for m in bm:
            m.sent()
        for m in xms:
            m.sent()
        lm(slot).sent()
        return carry

    lax.fori_loop(0, STEPS, step, 0)
    for m in xsm:
        m.sent()
    apply_load((STEPS - 1) % 2)
    outs = [
        pltpu.make_async_copy(a, b, in_sem.at[i])
        for i, (a, b) in enumerate([
            (V, o_motion), (S, o_stress),
            (H.at[pl.ds(0, 16), pl.ds(0, own)], o_surf),
            (M.at[pl.ds(0, 16), pl.ds(0, own)], o_mom.at[0]),
            (N.at[pl.ds(0, 16), pl.ds(0, own)], o_mom.at[1]),
        ])
    ]
    for c in outs:
        c.start()
    for c in outs:
        c.wait()


def body(nx, ny, motion, stress, buoyancy, lame_first, lame_shear, surface, momentum, bathymetry, wet_mask):
    plane = motion.shape[2:]
    two = motion.shape[1:]
    ext = (24, surface.shape[1] + 128)

    def v(*shape):
        return pltpu.VMEM(shape, F32)

    scratch = [v(*stress.shape), v(*motion.shape)] + [v(*two)] * 3
    scratch += [v(*ext)] * 3 + [pltpu.VMEM(wet_mask.shape, jnp.int32)] + [v(*ext)] * 11
    scratch += [v(2, *plane), v(*plane), v(*two), v(*two), v(*two)]
    scratch += [v(*plane), v(2, *plane), v(*two), v(*two), v(*two)]
    scratch += [v(2, 88, 128)] * 4
    scratch += [v(2, 16, ext[1])] * 4 + [v(16, ext[1])] * 4
    scratch += [v(2, 8, 128), v(2, 8, 128), v(8, 256)]
    dma = pltpu.SemaphoreType.DMA
    scratch += [dma((10,)), dma((12,)), dma((12,)), dma((2, 2)), dma((2, 2)), dma((2, 2)), dma((2, 2)), dma((2,)), dma((2,))]
    any_ = pl.BlockSpec(memory_space=pl.ANY)
    return pl.pallas_call(
        functools.partial(kernel, nx, ny),
        out_shape=[
            jax.ShapeDtypeStruct(a.shape, F32) for a in (motion, stress, surface, momentum)
        ],
        in_specs=[any_] * 9,
        out_specs=[any_] * 4,
        scratch_shapes=scratch,
        compiler_params=pltpu.CompilerParams(
            collective_id=0, has_side_effects=True, vmem_limit_bytes=32 * 1024 * 1024
        ),
        name="coupled",
    )(motion, stress, buoyancy, lame_first, lame_shear, surface, momentum, bathymetry, wet_mask)


def solution(mesh):
    return jax.shard_map(
        functools.partial(body, mesh.shape["gx"], mesh.shape["gy"]),
        mesh=mesh,
        in_specs=(
            P(None, "gx", None, "gy"),
            P(None, "gx", None, "gy"),
            P("gx", None, "gy"),
            P("gx", None, "gy"),
            P("gx", None, "gy"),
            P("gx", "gy"),
            P(None, "gx", "gy"),
            P("gx", "gy"),
            P("gx", "gy"),
        ),
        out_specs=(
            P(None, "gx", None, "gy"),
            P(None, "gx", None, "gy"),
            P("gx", "gy"),
            P(None, "gx", "gy"),
        ),
        check_vma=False,
    )
```

```python
import functools

import jax
import jax.numpy as jnp
from jax import lax
from jax.experimental import pallas as pl
from jax.experimental.pallas import tpu as pltpu
from jax.sharding import PartitionSpec as P

RATIO = 8
STEPS = 4
NSUB = 4
PARTS = 2
SOLID_STEP = 0.2
WAVE_STEP = 0.1
VISCOSITY = 0.05
UPLIFT_GAIN = 0.25
LOAD_GAIN = 8.0

MESH = pl.DeviceIdType.MESH
F32 = jnp.float32


def kernel(
    nx, ny,
    motion, stress, buoy, lame1, lame2, surf, mom, bath, wetm,
    o_motion, o_stress, o_surf, o_mom,
    S, V, Bu, L1, L2, H, M, N, Wi, W, D, wt, Dx, Dy, Ax, Bx, Ay, By, Fx, Up,
    hb_s, ha_xx, hd_s, hu_yy,
    hb_vx, ha_v, hd_vy, hu_v,
    cu, cd, hd_c, hu_c, csu, csd, hd_cs, hu_cs,
    xf, xb, hb_x, ha_x, xsf, xsb, hb_xs, ha_xs,
    ls, lr, tops,
    in_sem, send, recv, csend, crecv, xsend, xrecv, lsend, lrecv,
):
    gx = lax.axis_index("gx")
    gy = lax.axis_index("gy")
    has_b, has_a, has_d, has_u = gx > 0, gx < nx - 1, gy > 0, gy < ny - 1
    ahead = (jnp.minimum(gx + 1, nx - 1), gy)
    behind = (jnp.maximum(gx - 1, 0), gy)
    up = (gx, jnp.minimum(gy + 1, ny - 1))
    down = (gx, jnp.maximum(gy - 1, 0))
    dirs = {
        "f": (ahead, has_a, has_b),
        "b": (behind, has_b, has_a),
        "u": (up, has_u, has_d),
        "d": (down, has_d, has_u),
    }
    zdim = S.shape[2]
    lanes = H.shape[1]
    own = surf.shape[1]
    nt = lanes // 128

    loads = [
        pltpu.make_async_copy(a, b, in_sem.at[i])
        for i, (a, b) in enumerate([
            (wetm, Wi),
            (bath, D.at[pl.ds(0, 16), pl.ds(0, own)]),
            (surf, H.at[pl.ds(0, 16), pl.ds(0, own)]),
            (mom.at[0], M.at[pl.ds(0, 16), pl.ds(0, own)]),
            (mom.at[1], N.at[pl.ds(0, 16), pl.ds(0, own)]),
            (motion.at[pl.ds(1, 2)], V.at[pl.ds(0, 2)]), (motion.at[0], V.at[2]),
            (stress.at[pl.ds(0, 3)], S.at[pl.ds(0, 3)]), (stress.at[3], S.at[4]),
            (stress.at[4], S.at[3]), (stress.at[5], S.at[5]),
            (buoy, Bu), (lame1, L1), (lame2, L2),
        ])
    ]
    for c in loads:
        c.start()

    def zero_when_absent(flag, refs):
        @pl.when(jnp.logical_not(flag))
        def _():
            for r in refs:
                r[...] = jnp.zeros(r.shape, F32)

    zero_when_absent(has_b, [hb_s, hb_vx, hb_x, hb_xs])
    zero_when_absent(has_a, [ha_xx, ha_v, ha_x, ha_xs, lr])
    zero_when_absent(has_d, [hd_s, hd_vy, hd_c, hd_cs])
    zero_when_absent(has_u, [hu_yy, hu_v, hu_c, hu_cs])
    for r in (xf, xb, xsf, xsb, ls, tops):
        r[...] = jnp.zeros(r.shape, F32)

    barrier = pltpu.get_barrier_semaphore()
    for d in "fbud":
        dev, ok, _ = dirs[d]

        @pl.when(ok)
        def _():
            pl.semaphore_signal(barrier, inc=1, device_id=dev, device_id_type=MESH)

    pl.semaphore_wait(barrier, sum(f.astype(jnp.int32) for f in (has_b, has_a, has_d, has_u)))

    class Msg:
        def __init__(self, d, src, dst, ssem, rsem):
            dev, self.ok, self.inc = dirs[d]
            self.c = pltpu.make_async_remote_copy(
                src_ref=src, dst_ref=dst, send_sem=ssem, recv_sem=rsem,
                device_id=dev, device_id_type=MESH)

        def start(self):
            pl.when(self.ok)(lambda: self.c.start())

        def sent(self):
            pl.when(self.ok)(lambda: self.c.wait_send())

        def got(self):
            pl.when(self.inc)(lambda: self.c.wait_recv())

    count = [0]

    def msg(d, src, dst):
        i = count[0]
        count[0] += 1
        return Msg(d, src, dst, send.at[i], recv.at[i])

    size = zdim // PARTS
    am, bm = [], []
    for p in range(PARTS):
        zs = pl.ds(p * size, size)
        am.append([
            msg("f", S.at[pl.ds(3, 2), 1, zs], hb_s.at[:, zs]),
            msg("b", S.at[0, 0, zs], ha_xx.at[zs]),
            msg("u", S.at[pl.ds(4, 2), :, zs], hd_s.at[:, :, zs]),
            msg("d", S.at[1, :, zs], hu_yy.at[:, zs]),
        ])
        bm.append([
            msg("f", V.at[2, 1, zs], hb_vx.at[zs]),
            msg("b", V.at[pl.ds(0, 2), 0, zs], ha_v.at[:, zs]),
            msg("u", V.at[0, :, zs], hd_vy.at[:, zs]),
            msg("d", V.at[pl.ds(1, 2), :, zs], hu_v.at[:, :, zs]),
        ])
    csm = [msg("u", csu, hd_cs), msg("d", csd, hu_cs)]
    xsm = [msg("f", xsf, hb_xs), msg("b", xsb, ha_xs)]

    def xm(slot):
        return [
            Msg("f", xf.at[slot], hb_x.at[slot], xsend.at[0, slot], xrecv.at[0, slot]),
            Msg("b", xb.at[slot], ha_x.at[slot], xsend.at[1, slot], xrecv.at[1, slot]),
        ]

    def cm(slot):
        return [
            Msg("u", cu.at[slot], hd_c.at[slot], csend.at[0, slot], crecv.at[0, slot]),
            Msg("d", cd.at[slot], hu_c.at[slot], csend.at[1, slot], crecv.at[1, slot]),
        ]

    def lm(slot):
        return Msg("b", ls.at[slot], lr.at[slot], lsend.at[slot], lrecv.at[slot])

    lane = lax.broadcasted_iota(jnp.int32, (size, 128), 1)
    zrow = lax.broadcasted_iota(jnp.int32, (size, 128), 0)
    lane24 = lax.broadcasted_iota(jnp.int32, (24, 128), 1)
    lane8 = lax.broadcasted_iota(jnp.int32, (8, 128), 1)

    def ym(p, halo):
        return pltpu.roll(jnp.where(lane == 127, halo, p), 1, 1)

    def yp(p, halo):
        return pltpu.roll(jnp.where(lane == 0, halo, p), 127, 1)

    def zm(ref, c, x, z):
        if z == 0:
            return jnp.where(zrow == 0, 0.0, pltpu.roll(ref[c, x, 0:size, :], 1, 0))
        return pltpu.roll(ref[c, x, z - 8:z + size, :], 1, 0)[8:]

    def zp(ref, c, x, z):
        if z + size == zdim:
            return jnp.where(zrow == size - 1, 0.0, pltpu.roll(ref[c, x, z:zdim, :], size - 1, 0))
        return pltpu.roll(ref[c, x, z:z + size + 8, :], size + 7, 0)[:size]

    def rm(a):
        return pltpu.roll(a, 1, 0)

    def rp(a):
        return pltpu.roll(a, a.shape[0] - 1, 0)

    def cmn(a):
        return pltpu.roll(a, 1, 1)

    def cpl(a):
        return pltpu.roll(a, a.shape[1] - 1, 1)

    half = own // 2

    def fill_x(slot):
        for buf, rows in ((xf, slice(12, 16)), (xb, slice(0, 4))):
            buf[slot, 0:4, 0:own] = H[rows, 0:own]
            buf[slot, 4:8, 0:own] = M[rows, 0:own]
            buf[slot, 0:4, own:own + half] = N[rows, 0:half]
            buf[slot, 4:8, own:own + half] = N[rows, half:own]
        t = jnp.concatenate([V[1, 0, 0:1, :], V[1, 1, 0:1, :]], axis=0)
        xf[slot, 0:2, own + half:own + half + 128] = t
        tops[1:3, 0:128] = t

    def use_x(slot):
        at, left, right = slice(0, own), slice(0, half), slice(half, own)
        n = slice(own, own + half)
        a, b = ha_x, hb_x
        H[16:24, at] = jnp.concatenate([a[slot, 0:4, at], b[slot, 0:4, at]], axis=0)
        M[16:24, at] = jnp.concatenate([a[slot, 4:8, at], b[slot, 4:8, at]], axis=0)
        N[16:24, left] = jnp.concatenate([a[slot, 0:4, n], b[slot, 0:4, n]], axis=0)
        N[16:24, right] = jnp.concatenate([a[slot, 4:8, n], b[slot, 4:8, n]], axis=0)
        t = b[slot, 0:2, own + half:own + half + 128]
        tops[0:1, 0:128] = t[1:2, :]
        tops[3:4, 0:128] = t[0:1, :]

    def fill_c(slot):
        for i, r in enumerate((H, M, N)):
            cu[slot, 24 * i:24 * i + 24, :] = r[:, own - 128:own]
            cd[slot, 24 * i:24 * i + 24, :] = r[:, 0:128]
        cu[slot, 72:80, :] = tops[:, 0:128]
        cd[slot, 72:80, :] = tops[:, 0:128]

    def use_c(slot):
        for i, r in enumerate((H, M, N)):
            at = slice(24 * i, 24 * i + 24)
            r[:, own:lanes] = jnp.where(lane24 < 64, hu_c[slot, at, :], hd_c[slot, at, :])
        tops[:, 128:256] = jnp.where(
            lane8 < 8, hu_c[slot, 72:80, :], pltpu.roll(hd_c[slot, 72:80, :], 16, 1))

    def start_all(ms):
        for m in ms:
            m.start()

    for c in loads[7:11]:
        c.wait()
    for p in range(PARTS):
        start_all(am[p])
    for c in loads[:7]:
        c.wait()
    W[0:16, 0:own] = Wi[...].astype(F32)
    for buf, rows in ((xsf, slice(12, 16)), (xsb, slice(0, 4))):
        buf[0:4, 0:own] = W[rows, 0:own]
        buf[4:8, 0:own] = D[rows, 0:own]
    for q in range(own // 128):
        xsb[q:q + 1, own:own + 128] = W[4:5, 128 * q:128 * q + 128]
    fill_x(0)
    start_all(xm(0))
    start_all(xsm)
    for c in loads[11:]:
        c.wait()

    def bed_x():
        at = slice(0, own)
        W[16:24, at] = jnp.concatenate([ha_xs[0:4, at], hb_xs[0:4, at]], axis=0)
        D[16:24, at] = jnp.concatenate([ha_xs[4:8, at], hb_xs[4:8, at]], axis=0)
        w = W[:, at]
        Fx[:, at] = w * rp(w)
        nextw = jnp.concatenate(
            [ha_xs[q:q + 1, own:own + 128] for q in range(own // 128)], axis=1)
        Fx[16:20, at] = W[16:20, at] * jnp.concatenate([W[17:20, at], nextw], axis=0)
        for i, r in enumerate((W, D, Fx)):
            csu[24 * i:24 * i + 24, :] = r[:, own - 128:own]
            csd[24 * i:24 * i + 24, :] = r[:, 0:128]

    def ocean_setup():
        for i, r in enumerate((W, D, Fx)):
            at = slice(24 * i, 24 * i + 24)
            r[:, own:lanes] = jnp.where(lane24 < 64, hu_cs[at, :], hd_cs[at, :])
        w = W[...]
        d = D[...]
        fx = Fx[...]
        fy = w * cpl(w)
        wt[...] = WAVE_STEP * w
        Dx[...] = d + rp(d)
        Dy[...] = d + cpl(d)
        Bx[...] = VISCOSITY * fx
        By[...] = VISCOSITY * fy
        Ax[...] = fx * (1.0 - VISCOSITY * (rp(fx) + rm(fx) + cpl(fx) + cmn(fx)))
        Ay[...] = fy * (1.0 - VISCOSITY * (rp(fy) + rm(fy) + cpl(fy) + cmn(fy)))

    def mask_flow():
        fx = Fx[...]
        fy = W[...] * cpl(W[...])
        m, n = M[...], N[...]
        mm, nn = fx * m, fy * n
        dm, dn = m - mm, n - nn
        H[...] = H[...] - wt[...] * ((dm - rm(dm)) + (dn - cmn(dn)))
        M[...] = mm
        N[...] = nn

    def substep(_, carry):
        m, n = M[...], N[...]
        mw, ns = rm(m), cmn(n)
        h = H[...] - wt[...] * ((m - mw) + (n - ns))
        H[...] = h
        he, hn = rp(h), cpl(h)
        M[...] = Ax[...] * m + Bx[...] * (
            ((rp(m) + mw) + (cpl(m) + cmn(m))) - (Dx[...] + h + he) * (he - h))
        N[...] = Ay[...] * n + By[...] * (
            ((rp(n) + rm(n)) + (cpl(n) + ns)) - (Dy[...] + h + hn) * (hn - h))
        return carry

    er = lax.broadcasted_iota(jnp.int32, (128, 128), 0)
    ec = lax.broadcasted_iota(jnp.int32, (128, 128), 1)
    row24 = lax.broadcasted_iota(jnp.int32, (24, 128), 0)

    def lift():
        t = tops[:, 0:128]
        tiles = [t] + [pltpu.roll(t, 128 - 16 * q, 1) for q in range(1, nt - 1)]
        tiles.append(tops[:, 128:256])
        spread = jnp.where((ec // RATIO) == er, 1.0, 0.0)
        u = jnp.dot(jnp.concatenate(tiles, axis=0), spread,
                    preferred_element_type=F32, precision=lax.Precision.HIGHEST)
        for q in range(nt):
            r = u[8 * q:8 * q + 8, :]
            e = [jnp.broadcast_to(r[i:i + 1, :], (24, 128)) for i in range(4)]
            full = jnp.where(row24 < 8, e[0], jnp.where(row24 < 16, e[1], jnp.where(row24 < 20, e[2], e[3])))
            at = slice(128 * q, 128 * q + 128)
            Up[:, at] = full
        H[...] = H[...] + UPLIFT_GAIN * W[...] * Up[...]

    def average(slot):
        p = W[0:16, 0:own] * H[0:16, 0:own]
        parts = [p[:, 128 * q:128 * q + 128] for q in range(nt - 1)]
        gather = jnp.where((er // RATIO) == ec, 1.0, 0.0)
        g = jnp.dot(jnp.concatenate(parts, axis=0), gather,
                    preferred_element_type=F32, precision=lax.Precision.HIGHEST)
        a0 = jnp.zeros((1, 128), F32)
        a1 = jnp.zeros((1, 128), F32)
        for q in range(nt - 1):
            s0 = jnp.sum(g[16 * q:16 * q + 8, :], axis=0, keepdims=True)
            s1 = jnp.sum(g[16 * q + 8:16 * q + 16, :], axis=0, keepdims=True)
            two = jnp.concatenate([s0, s1, jnp.zeros((6, 128), F32)], axis=0)
            if q:
                two = pltpu.roll(two, 16 * q, 1)
            a0 = a0 + two[0:1, :]
            a1 = a1 + two[1:2, :]
        scale = -LOAD_GAIN / (RATIO * RATIO)
        ls[slot, 0:1, :] = a0 * scale
        ls[slot, 1:2, :] = a1 * scale

    def apply_load(slot):
        lm(slot).got()
        S[2, 0, 0:1, :] = ls[slot, 1:2, :]
        S[2, 1, 0:1, :] = lr[slot, 0:1, :]

    def motion_part(z):
        zs = slice(z, z + size)
        for x in range(2):
            sb = SOLID_STEP * Bu[x, zs]
            xx, yy, zz, xz, xy, yz = (S[c, x, zs] for c in range(6))
            xx_a = S[0, 1, zs] if x == 0 else ha_xx[zs]
            xz_b = hb_s[0, zs] if x == 0 else S[3, 0, zs]
            xy_b = hb_s[1, zs] if x == 0 else S[4, 0, zs]
            V[2, x, zs] = V[2, x, zs] + sb * (
                (xx_a - xx) + (xy - ym(xy, hd_s[0, x, zs])) + (xz - zm(S, 3, x, z)))
            V[0, x, zs] = V[0, x, zs] + sb * (
                (xy - xy_b) + (yp(yy, hu_yy[x, zs]) - yy) + (yz - zm(S, 5, x, z)))
            V[1, x, zs] = V[1, x, zs] + sb * (
                (xz - xz_b) + (yz - ym(yz, hd_s[1, x, zs])) + (zp(S, 2, x, z) - zz))

    def stress_part(z):
        zs = slice(z, z + size)
        for x in range(2):
            vy, vz, vx = V[0, x, zs], V[1, x, zs], V[2, x, zs]
            vx_b = hb_vx[zs] if x == 0 else V[2, 0, zs]
            vy_a = V[0, 1, zs] if x == 0 else ha_v[0, zs]
            vz_a = V[1, 1, zs] if x == 0 else ha_v[1, zs]
            ex = vx - vx_b
            ey = vy - ym(vy, hd_vy[x, zs])
            ez = vz - zm(V, 1, x, z)
            l, g = SOLID_STEP * L1[x, zs], SOLID_STEP * L2[x, zs]
            tr = l * (ex + ey + ez)
            g2 = 2.0 * g
            S[0, x, zs] = S[0, x, zs] + (tr + g2 * ex)
            S[1, x, zs] = S[1, x, zs] + (tr + g2 * ey)
            S[2, x, zs] = S[2, x, zs] + (tr + g2 * ez)
            S[3, x, zs] = S[3, x, zs] + g * ((zp(V, 2, x, z) - vx) + (vz_a - vz))
            S[4, x, zs] = S[4, x, zs] + g * ((yp(vx, hu_v[1, x, zs]) - vx) + (vy_a - vy))
            S[5, x, zs] = S[5, x, zs] + g * ((zp(V, 0, x, z) - vy) + (yp(vz, hu_v[0, x, zs]) - vz))

    def step(k, carry):
        slot = lax.rem(k, 2)
        nslot = lax.rem(k + 1, 2)

        xms = xm(slot)
        cms = cm(slot)
        for m in xms:
            m.got()
        use_x(slot)

        @pl.when(k == 0)
        def _():
            for m in xsm:
                m.got()
            bed_x()
            start_all(csm)

        fill_c(slot)
        start_all(cms)

        for p in range(PARTS):
            for m in am[p]:
                m.got()
            if p == 0:
                @pl.when(k > 0)
                def _():
                    apply_load(nslot)

            motion_part(p * size)
            start_all(bm[p])

        for m in cms:
            m.got()
        use_c(slot)

        @pl.when(k == 0)
        def _():
            for m in csm:
                m.got()
            ocean_setup()
            mask_flow()

        lift()
        lax.fori_loop(0, NSUB, substep, 0)
        average(slot)
        lm(slot).start()

        @pl.when(k < STEPS - 1)
        def _():
            fill_x(nslot)
            start_all(xm(nslot))

        for p in range(PARTS):
            for m in bm[p]:
                m.got()
            for m in am[p]:
                m.sent()
            stress_part(p * size)

            @pl.when(k < STEPS - 1)
            def _():
                start_all(am[p])

        for ms in bm:
            for m in ms:
                m.sent()
        for m in xms + cms:
            m.sent()
        lm(slot).sent()
        return carry

    lax.fori_loop(0, STEPS, step, 0)
    for m in xsm + csm:
        m.sent()
    apply_load((STEPS - 1) % 2)
    outs = [
        pltpu.make_async_copy(a, b, in_sem.at[i])
        for i, (a, b) in enumerate([
            (V.at[pl.ds(0, 2)], o_motion.at[pl.ds(1, 2)]), (V.at[2], o_motion.at[0]),
            (S.at[pl.ds(0, 3)], o_stress.at[pl.ds(0, 3)]), (S.at[4], o_stress.at[3]),
            (S.at[3], o_stress.at[4]), (S.at[5], o_stress.at[5]),
            (H.at[pl.ds(0, 16), pl.ds(0, own)], o_surf),
            (M.at[pl.ds(0, 16), pl.ds(0, own)], o_mom.at[0]),
            (N.at[pl.ds(0, 16), pl.ds(0, own)], o_mom.at[1]),
        ])
    ]
    for c in outs:
        c.start()
    for c in outs:
        c.wait()


def body(nx, ny, motion, stress, buoyancy, lame_first, lame_shear, surface, momentum, bathymetry, wet_mask):
    plane = motion.shape[2:]
    two = motion.shape[1:]
    ext = (24, surface.shape[1] + 128)

    def v(*shape):
        return pltpu.VMEM(shape, F32)

    scratch = [v(*stress.shape), v(*motion.shape)] + [v(*two)] * 3
    scratch += [v(*ext)] * 3 + [pltpu.VMEM(wet_mask.shape, jnp.int32)] + [v(*ext)] * 11
    scratch += [v(2, *plane), v(*plane), v(2, *two), v(*two)]
    scratch += [v(*plane), v(2, *plane), v(*two), v(2, *two)]
    scratch += [v(2, 80, 128)] * 4 + [v(72, 128)] * 4
    wide = surface.shape[1]
    scratch += [v(2, 8, wide + wide // 2 + 128)] * 4 + [v(8, wide + 128)] * 4
    scratch += [v(2, 8, 128), v(2, 8, 128), v(8, 256)]
    dma = pltpu.SemaphoreType.DMA
    scratch += [dma((14,)), dma((8 * PARTS + 4,)), dma((8 * PARTS + 4,)), dma((2, 2)), dma((2, 2)), dma((2, 2)), dma((2, 2)), dma((2,)), dma((2,))]
    return pl.pallas_call(
        functools.partial(kernel, nx, ny),
        out_shape=[
            jax.ShapeDtypeStruct(a.shape, F32) for a in (motion, stress, surface, momentum)
        ],
        in_specs=[pl.BlockSpec(memory_space=pltpu.HBM)] * 9,
        out_specs=[pl.BlockSpec(memory_space=pltpu.HBM)] * 4,
        scratch_shapes=scratch,
        compiler_params=pltpu.CompilerParams(
            collective_id=0, has_side_effects=True, vmem_limit_bytes=60 * 1024 * 1024
        ),
        name="coupled",
    )(motion, stress, buoyancy, lame_first, lame_shear, surface, momentum, bathymetry, wet_mask)


def solution(mesh):
    return jax.shard_map(
        functools.partial(body, mesh.shape["gx"], mesh.shape["gy"]),
        mesh=mesh,
        in_specs=(
            P(None, "gx", None, "gy"),
            P(None, "gx", None, "gy"),
            P("gx", None, "gy"),
            P("gx", None, "gy"),
            P("gx", None, "gy"),
            P("gx", "gy"),
            P(None, "gx", "gy"),
            P("gx", "gy"),
            P("gx", "gy"),
        ),
        out_specs=(
            P(None, "gx", None, "gy"),
            P(None, "gx", None, "gy"),
            P("gx", "gy"),
            P(None, "gx", "gy"),
        ),
        check_vma=False,
    )
```

```python
import functools

import jax
import jax.numpy as jnp
from jax import lax
from jax.experimental import pallas as pl
from jax.experimental.pallas import tpu as pltpu
from jax.sharding import PartitionSpec as P

RATIO = 8
STEPS = 4
NSUB = 4
PARTS = 2
SOLID_STEP = 0.2
WAVE_STEP = 0.1
VISCOSITY = 0.05
UPLIFT_GAIN = 0.25
LOAD_GAIN = 8.0

MESH = pl.DeviceIdType.MESH
F32 = jnp.float32


def kernel(
    nx, ny,
    motion, stress, buoy, lame1, lame2, surf, mom, bath, wetm,
    V, S, H, M, N,
    Bu, L1, L2, Wi, W, D, wt, Dx, Dy, Ax, Bx, Ay, By, Fx, Up,
    hb_s, ha_xx, hd_s, hu_yy,
    hb_vx, ha_v, hd_vy, hu_v,
    cu, cd, hd_c, hu_c, csu, csd, hd_cs, hu_cs,
    xf, xb, hb_x, ha_x, xsf, xsb, hb_xs, ha_xs,
    ls, lr, tops,
    in_sem, send, recv, csend, crecv, xsend, xrecv, lsend, lrecv,
):
    gx = lax.axis_index("gx")
    gy = lax.axis_index("gy")
    has_b, has_a, has_d, has_u = gx > 0, gx < nx - 1, gy > 0, gy < ny - 1
    ahead = (jnp.minimum(gx + 1, nx - 1), gy)
    behind = (jnp.maximum(gx - 1, 0), gy)
    up = (gx, jnp.minimum(gy + 1, ny - 1))
    down = (gx, jnp.maximum(gy - 1, 0))
    dirs = {
        "f": (ahead, has_a, has_b),
        "b": (behind, has_b, has_a),
        "u": (up, has_u, has_d),
        "d": (down, has_d, has_u),
    }
    zdim = S.shape[2]
    lanes = H.shape[1]
    own = surf.shape[1]
    nt = lanes // 128

    loads = [
        pltpu.make_async_copy(a, b, in_sem.at[i])
        for i, (a, b) in enumerate([
            (wetm, Wi),
            (bath, D.at[pl.ds(0, 16), pl.ds(0, own)]),
            (surf, H.at[pl.ds(0, 16), pl.ds(0, own)]),
            (mom.at[0], M.at[pl.ds(0, 16), pl.ds(0, own)]),
            (mom.at[1], N.at[pl.ds(0, 16), pl.ds(0, own)]),
            (motion.at[pl.ds(1, 2)], V.at[pl.ds(0, 2)]), (motion.at[0], V.at[2]),
            (stress.at[pl.ds(0, 3)], S.at[pl.ds(0, 3)]), (stress.at[3], S.at[4]),
            (stress.at[4], S.at[3]), (stress.at[5], S.at[5]),
            (buoy, Bu), (lame1, L1), (lame2, L2),
        ])
    ]
    for c in loads:
        c.start()

    def zero_when_absent(flag, refs):
        @pl.when(jnp.logical_not(flag))
        def _():
            for r in refs:
                r[...] = jnp.zeros(r.shape, F32)

    zero_when_absent(has_b, [hb_s, hb_vx, hb_x, hb_xs])
    zero_when_absent(has_a, [ha_xx, ha_v, ha_x, ha_xs, lr])
    zero_when_absent(has_d, [hd_s, hd_vy, hd_c, hd_cs])
    zero_when_absent(has_u, [hu_yy, hu_v, hu_c, hu_cs])
    for r in (xf, xb, xsf, xsb, ls, tops):
        r[...] = jnp.zeros(r.shape, F32)

    barrier = pltpu.get_barrier_semaphore()
    for d in "fbud":
        dev, ok, _ = dirs[d]

        @pl.when(ok)
        def _():
            pl.semaphore_signal(barrier, inc=1, device_id=dev, device_id_type=MESH)

    pl.semaphore_wait(barrier, sum(f.astype(jnp.int32) for f in (has_b, has_a, has_d, has_u)))

    class Msg:
        def __init__(self, d, src, dst, ssem, rsem):
            dev, self.ok, self.inc = dirs[d]
            self.c = pltpu.make_async_remote_copy(
                src_ref=src, dst_ref=dst, send_sem=ssem, recv_sem=rsem,
                device_id=dev, device_id_type=MESH)

        def start(self):
            pl.when(self.ok)(lambda: self.c.start())

        def sent(self):
            pl.when(self.ok)(lambda: self.c.wait_send())

        def got(self):
            pl.when(self.inc)(lambda: self.c.wait_recv())

    count = [0]

    def msg(d, src, dst):
        i = count[0]
        count[0] += 1
        return Msg(d, src, dst, send.at[i], recv.at[i])

    size = zdim // PARTS
    am, bm = [], []
    for p in range(PARTS):
        zs = pl.ds(p * size, size)
        am.append([
            msg("f", S.at[pl.ds(3, 2), 1, zs], hb_s.at[:, zs]),
            msg("b", S.at[0, 0, zs], ha_xx.at[zs]),
            msg("u", S.at[pl.ds(4, 2), :, zs], hd_s.at[:, :, zs]),
            msg("d", S.at[1, :, zs], hu_yy.at[:, zs]),
        ])
        bm.append([
            msg("f", V.at[2, 1, zs], hb_vx.at[zs]),
            msg("b", V.at[pl.ds(0, 2), 0, zs], ha_v.at[:, zs]),
            msg("u", V.at[0, :, zs], hd_vy.at[:, zs]),
            msg("d", V.at[pl.ds(1, 2), :, zs], hu_v.at[:, :, zs]),
        ])
    csm = [msg("u", csu, hd_cs), msg("d", csd, hu_cs)]
    xsm = [msg("f", xsf, hb_xs), msg("b", xsb, ha_xs)]

    def xm(slot):
        return [
            Msg("f", xf.at[slot], hb_x.at[slot], xsend.at[0, slot], xrecv.at[0, slot]),
            Msg("b", xb.at[slot], ha_x.at[slot], xsend.at[1, slot], xrecv.at[1, slot]),
        ]

    def cm(slot):
        return [
            Msg("u", cu.at[slot], hd_c.at[slot], csend.at[0, slot], crecv.at[0, slot]),
            Msg("d", cd.at[slot], hu_c.at[slot], csend.at[1, slot], crecv.at[1, slot]),
        ]

    def lm(slot):
        return Msg("b", ls.at[slot], lr.at[slot], lsend.at[slot], lrecv.at[slot])

    lane = lax.broadcasted_iota(jnp.int32, (size, 128), 1)
    zrow = lax.broadcasted_iota(jnp.int32, (size, 128), 0)
    lane24 = lax.broadcasted_iota(jnp.int32, (24, 128), 1)
    lane8 = lax.broadcasted_iota(jnp.int32, (8, 128), 1)

    def ym(p, halo):
        return pltpu.roll(jnp.where(lane == 127, halo, p), 1, 1)

    def yp(p, halo):
        return pltpu.roll(jnp.where(lane == 0, halo, p), 127, 1)

    def zm(ref, c, x, z):
        if z == 0:
            return jnp.where(zrow == 0, 0.0, pltpu.roll(ref[c, x, 0:size, :], 1, 0))
        return pltpu.roll(ref[c, x, z - 8:z + size, :], 1, 0)[8:]

    def zp(ref, c, x, z):
        if z + size == zdim:
            return jnp.where(zrow == size - 1, 0.0, pltpu.roll(ref[c, x, z:zdim, :], size - 1, 0))
        return pltpu.roll(ref[c, x, z:z + size + 8, :], size + 7, 0)[:size]

    def rm(a):
        return pltpu.roll(a, 1, 0)

    def rp(a):
        return pltpu.roll(a, a.shape[0] - 1, 0)

    def cmn(a):
        return pltpu.roll(a, 1, 1)

    def cpl(a):
        return pltpu.roll(a, a.shape[1] - 1, 1)

    half = own // 2

    def fill_x(slot):
        for buf, rows in ((xf, slice(12, 16)), (xb, slice(0, 4))):
            buf[slot, 0:4, 0:own] = H[rows, 0:own]
            buf[slot, 4:8, 0:own] = M[rows, 0:own]
            buf[slot, 0:4, own:own + half] = N[rows, 0:half]
            buf[slot, 4:8, own:own + half] = N[rows, half:own]
        t = jnp.concatenate([V[1, 0, 0:1, :], V[1, 1, 0:1, :]], axis=0)
        xf[slot, 0:2, own + half:own + half + 128] = t
        tops[1:3, 0:128] = t

    def use_x(slot):
        at, left, right = slice(0, own), slice(0, half), slice(half, own)
        n = slice(own, own + half)
        a, b = ha_x, hb_x
        H[16:24, at] = jnp.concatenate([a[slot, 0:4, at], b[slot, 0:4, at]], axis=0)
        M[16:24, at] = jnp.concatenate([a[slot, 4:8, at], b[slot, 4:8, at]], axis=0)
        N[16:24, left] = jnp.concatenate([a[slot, 0:4, n], b[slot, 0:4, n]], axis=0)
        N[16:24, right] = jnp.concatenate([a[slot, 4:8, n], b[slot, 4:8, n]], axis=0)
        t = b[slot, 0:2, own + half:own + half + 128]
        tops[0:1, 0:128] = t[1:2, :]
        tops[3:4, 0:128] = t[0:1, :]

    def fill_c(slot):
        for i, r in enumerate((H, M, N)):
            cu[slot, 24 * i:24 * i + 24, :] = r[:, own - 128:own]
            cd[slot, 24 * i:24 * i + 24, :] = r[:, 0:128]
        cu[slot, 72:80, :] = tops[:, 0:128]
        cd[slot, 72:80, :] = tops[:, 0:128]

    def use_c(slot):
        for i, r in enumerate((H, M, N)):
            at = slice(24 * i, 24 * i + 24)
            r[:, own:lanes] = jnp.where(lane24 < 64, hu_c[slot, at, :], hd_c[slot, at, :])
        tops[:, 128:256] = jnp.where(
            lane8 < 8, hu_c[slot, 72:80, :], pltpu.roll(hd_c[slot, 72:80, :], 16, 1))

    def start_all(ms):
        for m in ms:
            m.start()

    for c in loads[7:11]:
        c.wait()
    for p in range(PARTS):
        start_all(am[p])
    for c in loads[:7]:
        c.wait()
    W[0:16, 0:own] = Wi[...].astype(F32)
    for buf, rows in ((xsf, slice(12, 16)), (xsb, slice(0, 4))):
        buf[0:4, 0:own] = W[rows, 0:own]
        buf[4:8, 0:own] = D[rows, 0:own]
    for q in range(own // 128):
        xsb[q:q + 1, own:own + 128] = W[4:5, 128 * q:128 * q + 128]
    fill_x(0)
    start_all(xm(0))
    start_all(xsm)
    for c in loads[11:]:
        c.wait()

    def bed_x():
        at = slice(0, own)
        W[16:24, at] = jnp.concatenate([ha_xs[0:4, at], hb_xs[0:4, at]], axis=0)
        D[16:24, at] = jnp.concatenate([ha_xs[4:8, at], hb_xs[4:8, at]], axis=0)
        w = W[:, at]
        Fx[:, at] = w * rp(w)
        nextw = jnp.concatenate(
            [ha_xs[q:q + 1, own:own + 128] for q in range(own // 128)], axis=1)
        Fx[16:20, at] = W[16:20, at] * jnp.concatenate([W[17:20, at], nextw], axis=0)
        for i, r in enumerate((W, D, Fx)):
            csu[24 * i:24 * i + 24, :] = r[:, own - 128:own]
            csd[24 * i:24 * i + 24, :] = r[:, 0:128]

    def ocean_setup():
        for i, r in enumerate((W, D, Fx)):
            at = slice(24 * i, 24 * i + 24)
            r[:, own:lanes] = jnp.where(lane24 < 64, hu_cs[at, :], hd_cs[at, :])
        w = W[...]
        d = D[...]
        fx = Fx[...]
        fy = w * cpl(w)
        wt[...] = WAVE_STEP * w
        Dx[...] = d + rp(d)
        Dy[...] = d + cpl(d)
        Bx[...] = VISCOSITY * fx
        By[...] = VISCOSITY * fy
        Ax[...] = fx * (1.0 - VISCOSITY * (rp(fx) + rm(fx) + cpl(fx) + cmn(fx)))
        Ay[...] = fy * (1.0 - VISCOSITY * (rp(fy) + rm(fy) + cpl(fy) + cmn(fy)))

    def mask_flow():
        fx = Fx[...]
        fy = W[...] * cpl(W[...])
        m, n = M[...], N[...]
        mm, nn = fx * m, fy * n
        dm, dn = m - mm, n - nn
        H[...] = H[...] - wt[...] * ((dm - rm(dm)) + (dn - cmn(dn)))
        M[...] = mm
        N[...] = nn

    def substep(_, carry):
        m, n = M[...], N[...]
        mw, ns = rm(m), cmn(n)
        h = H[...] - wt[...] * ((m - mw) + (n - ns))
        H[...] = h
        he, hn = rp(h), cpl(h)
        M[...] = Ax[...] * m + Bx[...] * (
            ((rp(m) + mw) + (cpl(m) + cmn(m))) - (Dx[...] + h + he) * (he - h))
        N[...] = Ay[...] * n + By[...] * (
            ((rp(n) + rm(n)) + (cpl(n) + ns)) - (Dy[...] + h + hn) * (hn - h))
        return carry

    er = lax.broadcasted_iota(jnp.int32, (128, 128), 0)
    ec = lax.broadcasted_iota(jnp.int32, (128, 128), 1)
    row24 = lax.broadcasted_iota(jnp.int32, (24, 128), 0)

    def spread_dot(a, ones):
        p0 = a.astype(jnp.bfloat16)
        r = a - p0.astype(F32)
        p1 = r.astype(jnp.bfloat16)
        p2 = (r - p1.astype(F32)).astype(jnp.bfloat16)
        e = ones.astype(jnp.bfloat16)
        return jnp.dot(jnp.concatenate([p0, p1, p2], axis=1),
                       jnp.concatenate([e, e, e], axis=0), preferred_element_type=F32)

    def lift():
        t = tops[:, 0:128]
        tiles = [t] + [pltpu.roll(t, 128 - 16 * q, 1) for q in range(1, nt - 1)]
        tiles.append(tops[:, 128:256])
        spread = jnp.where((ec // RATIO) == er, 1.0, 0.0)
        u = spread_dot(jnp.concatenate(tiles, axis=0), spread)
        for q in range(nt):
            r = u[8 * q:8 * q + 8, :]
            e = [jnp.broadcast_to(r[i:i + 1, :], (24, 128)) for i in range(4)]
            full = jnp.where(row24 < 8, e[0], jnp.where(row24 < 16, e[1], jnp.where(row24 < 20, e[2], e[3])))
            at = slice(128 * q, 128 * q + 128)
            Up[:, at] = full
        H[...] = H[...] + UPLIFT_GAIN * W[...] * Up[...]

    def average(slot):
        p = W[0:16, 0:own] * H[0:16, 0:own]
        parts = [p[:, 128 * q:128 * q + 128] for q in range(nt - 1)]
        gather = jnp.where((er // RATIO) == ec, 1.0, 0.0)
        g = spread_dot(jnp.concatenate(parts, axis=0), gather)
        a0, a1 = g[0:8, :], g[8:16, :]
        for q in range(1, nt - 1):
            a0 = a0 + pltpu.roll(g[16 * q:16 * q + 8, :], 16 * q, 1)
            a1 = a1 + pltpu.roll(g[16 * q + 8:16 * q + 16, :], 16 * q, 1)
        scale = -LOAD_GAIN / (RATIO * RATIO)
        ls[slot, 0:1, :] = jnp.sum(a0, axis=0, keepdims=True) * scale
        ls[slot, 1:2, :] = jnp.sum(a1, axis=0, keepdims=True) * scale
        lm(slot).start()

    def apply_load(slot):
        lm(slot).got()
        S[2, 0, 0:1, :] = ls[slot, 1:2, :]
        S[2, 1, 0:1, :] = lr[slot, 0:1, :]

    def motion_part(z):
        zs = slice(z, z + size)
        for x in range(2):
            sb = SOLID_STEP * Bu[x, zs]
            xx, yy, zz, xz, xy, yz = (S[c, x, zs] for c in range(6))
            xx_a = S[0, 1, zs] if x == 0 else ha_xx[zs]
            xz_b = hb_s[0, zs] if x == 0 else S[3, 0, zs]
            xy_b = hb_s[1, zs] if x == 0 else S[4, 0, zs]
            V[2, x, zs] = V[2, x, zs] + sb * (
                (xx_a - xx) + (xy - ym(xy, hd_s[0, x, zs])) + (xz - zm(S, 3, x, z)))
            V[0, x, zs] = V[0, x, zs] + sb * (
                (xy - xy_b) + (yp(yy, hu_yy[x, zs]) - yy) + (yz - zm(S, 5, x, z)))
            V[1, x, zs] = V[1, x, zs] + sb * (
                (xz - xz_b) + (yz - ym(yz, hd_s[1, x, zs])) + (zp(S, 2, x, z) - zz))

    def stress_part(z):
        zs = slice(z, z + size)
        for x in range(2):
            vy, vz, vx = V[0, x, zs], V[1, x, zs], V[2, x, zs]
            vx_b = hb_vx[zs] if x == 0 else V[2, 0, zs]
            vy_a = V[0, 1, zs] if x == 0 else ha_v[0, zs]
            vz_a = V[1, 1, zs] if x == 0 else ha_v[1, zs]
            ex = vx - vx_b
            ey = vy - ym(vy, hd_vy[x, zs])
            ez = vz - zm(V, 1, x, z)
            l, g = SOLID_STEP * L1[x, zs], SOLID_STEP * L2[x, zs]
            tr = l * (ex + ey + ez)
            g2 = 2.0 * g
            S[0, x, zs] = S[0, x, zs] + (tr + g2 * ex)
            S[1, x, zs] = S[1, x, zs] + (tr + g2 * ey)
            S[2, x, zs] = S[2, x, zs] + (tr + g2 * ez)
            S[3, x, zs] = S[3, x, zs] + g * ((zp(V, 2, x, z) - vx) + (vz_a - vz))
            S[4, x, zs] = S[4, x, zs] + g * ((yp(vx, hu_v[1, x, zs]) - vx) + (vy_a - vy))
            S[5, x, zs] = S[5, x, zs] + g * ((zp(V, 0, x, z) - vy) + (yp(vz, hu_v[0, x, zs]) - vz))

    def step(k, carry):
        slot = lax.rem(k, 2)
        nslot = lax.rem(k + 1, 2)

        xms = xm(slot)
        cms = cm(slot)
        for m in xms:
            m.got()
        use_x(slot)

        @pl.when(k == 0)
        def _():
            for m in xsm:
                m.got()
            bed_x()
            start_all(csm)

        fill_c(slot)
        start_all(cms)
        for m in cms:
            m.got()
        use_c(slot)

        @pl.when(k == 0)
        def _():
            for m in csm:
                m.got()
            ocean_setup()
            mask_flow()

        lift()

        for p in range(PARTS):
            for m in am[p]:
                m.got()
            if p == 0:
                @pl.when(k > 0)
                def _():
                    apply_load(nslot)

            motion_part(p * size)
            start_all(bm[p])
            lax.fori_loop(NSUB * p // PARTS, NSUB * (p + 1) // PARTS, substep, 0)

        last = k == STEPS - 1
        pl.when(last)(lambda: average(slot))

        @pl.when(k < STEPS - 1)
        def _():
            fill_x(nslot)
            start_all(xm(nslot))

        for p in range(PARTS):
            for m in bm[p]:
                m.got()
            for m in am[p]:
                m.sent()
            stress_part(p * size)

            @pl.when(k < STEPS - 1)
            def _():
                start_all(am[p])

        pl.when(jnp.logical_not(last))(lambda: average(slot))
        for ms in bm:
            for m in ms:
                m.sent()
        for m in xms + cms:
            m.sent()
        lm(slot).sent()
        return carry

    lax.fori_loop(0, STEPS, step, 0)
    for m in xsm + csm:
        m.sent()
    apply_load((STEPS - 1) % 2)


def write_out(V, S, H, M, N, o_motion, o_stress, o_surf, o_mom, sem):
    rows, own = o_surf.shape
    at = (pl.ds(0, rows), pl.ds(0, own))
    outs = [
        pltpu.make_async_copy(a, b, sem.at[i])
        for i, (a, b) in enumerate([
            (S.at[pl.ds(0, 3)], o_stress.at[pl.ds(0, 3)]),
            (V.at[pl.ds(0, 2)], o_motion.at[pl.ds(1, 2)]), (V.at[2], o_motion.at[0]),
            (S.at[4], o_stress.at[3]), (S.at[3], o_stress.at[4]), (S.at[5], o_stress.at[5]),
            (H.at[at], o_surf), (M.at[at], o_mom.at[0]), (N.at[at], o_mom.at[1]),
        ])
    ]
    for c in outs:
        c.start()
    for c in outs:
        c.wait()


def body(nx, ny, motion, stress, buoyancy, lame_first, lame_shear, surface, momentum, bathymetry, wet_mask):
    plane = motion.shape[2:]
    two = motion.shape[1:]
    ext = (24, surface.shape[1] + 128)

    def v(*shape):
        return pltpu.VMEM(shape, F32)

    scratch = [v(*two)] * 3 + [pltpu.VMEM(wet_mask.shape, jnp.int32)] + [v(*ext)] * 11
    scratch += [v(2, *plane), v(*plane), v(2, *two), v(*two)]
    scratch += [v(*plane), v(2, *plane), v(*two), v(2, *two)]
    scratch += [v(2, 80, 128)] * 4 + [v(72, 128)] * 4
    wide = surface.shape[1]
    scratch += [v(2, 8, wide + wide // 2 + 128)] * 4 + [v(8, wide + 128)] * 4
    scratch += [v(2, 8, 128), v(2, 8, 128), v(8, 256)]
    dma = pltpu.SemaphoreType.DMA
    scratch += [dma((14,)), dma((8 * PARTS + 4,)), dma((8 * PARTS + 4,)), dma((2, 2)), dma((2, 2)), dma((2, 2)), dma((2, 2)), dma((2,)), dma((2,))]
    state = [motion.shape, stress.shape, ext, ext, ext]
    hbm = pl.BlockSpec(memory_space=pltpu.HBM)
    held = pl.pallas_call(
        functools.partial(kernel, nx, ny),
        out_shape=[pltpu.VMEM(shape, F32) for shape in state],
        in_specs=[hbm] * 9,
        out_specs=[pl.BlockSpec(memory_space=pltpu.VMEM)] * 5,
        scratch_shapes=scratch,
        compiler_params=pltpu.CompilerParams(
            collective_id=0, has_side_effects=True, vmem_limit_bytes=56 * 1024 * 1024
        ),
        name="coupled",
    )(motion, stress, buoyancy, lame_first, lame_shear, surface, momentum, bathymetry, wet_mask)
    return pl.pallas_call(
        write_out,
        out_shape=[
            jax.ShapeDtypeStruct(a.shape, F32) for a in (motion, stress, surface, momentum)
        ],
        in_specs=[pl.BlockSpec(memory_space=pl.ANY)] * 5,
        out_specs=[pl.BlockSpec(memory_space=pl.ANY)] * 4,
        scratch_shapes=[dma((9,))],
        name="write_out",
    )(*held)


def solution(mesh):
    return jax.shard_map(
        functools.partial(body, mesh.shape["gx"], mesh.shape["gy"]),
        mesh=mesh,
        in_specs=(
            P(None, "gx", None, "gy"),
            P(None, "gx", None, "gy"),
            P("gx", None, "gy"),
            P("gx", None, "gy"),
            P("gx", None, "gy"),
            P("gx", "gy"),
            P(None, "gx", "gy"),
            P("gx", "gy"),
            P("gx", "gy"),
        ),
        out_specs=(
            P(None, "gx", None, "gy"),
            P(None, "gx", None, "gy"),
            P("gx", "gy"),
            P(None, "gx", "gy"),
        ),
        check_vma=False,
    )
```

```python
import functools

import jax
import jax.numpy as jnp
from jax import lax
from jax.experimental import pallas as pl
from jax.experimental.pallas import tpu as pltpu
from jax.sharding import PartitionSpec as P

RATIO = 8
STEPS = 4
NSUB = 4
PARTS = 2
SOLID_STEP = 0.2
WAVE_STEP = 0.1
VISCOSITY = 0.05
UPLIFT_GAIN = 0.25
LOAD_GAIN = 8.0

MESH = pl.DeviceIdType.MESH
F32 = jnp.float32


def kernel(
    nx, ny,
    motion, stress, buoy, lame1, lame2, surf, mom, bath, wetm,
    V, S, H, M, N,
    Bu, L1, L2, Wi, W, D, wt, Dx, Dy, Ax, Bx, Ay, By, Fx,
    hb_s, ha_xx, hd_s, hu_yy,
    hb_vx, ha_v, hd_vy, hu_v,
    cu, cd, hd_c, hu_c, csu, csd, hd_cs, hu_cs,
    xf, xb, hb_x, ha_x, xsf, xsb, hb_xs, ha_xs,
    ls, lr, tops,
    in_sem, send, recv, csend, crecv, xsend, xrecv, lsend, lrecv,
):
    gx = lax.axis_index("gx")
    gy = lax.axis_index("gy")
    has_b, has_a, has_d, has_u = gx > 0, gx < nx - 1, gy > 0, gy < ny - 1
    ahead = (jnp.minimum(gx + 1, nx - 1), gy)
    behind = (jnp.maximum(gx - 1, 0), gy)
    up = (gx, jnp.minimum(gy + 1, ny - 1))
    down = (gx, jnp.maximum(gy - 1, 0))
    dirs = {
        "f": (ahead, has_a, has_b),
        "b": (behind, has_b, has_a),
        "u": (up, has_u, has_d),
        "d": (down, has_d, has_u),
    }
    zdim = S.shape[2]
    lanes = H.shape[1]
    own = surf.shape[1]
    nt = lanes // 128

    loads = [
        pltpu.make_async_copy(a, b, in_sem.at[i])
        for i, (a, b) in enumerate([
            (wetm, Wi),
            (bath, D.at[pl.ds(0, 16), pl.ds(0, own)]),
            (surf, H.at[pl.ds(0, 16), pl.ds(0, own)]),
            (mom.at[0], M.at[pl.ds(0, 16), pl.ds(0, own)]),
            (mom.at[1], N.at[pl.ds(0, 16), pl.ds(0, own)]),
            (motion.at[pl.ds(1, 2)], V.at[pl.ds(0, 2)]), (motion.at[0], V.at[2]),
            (stress.at[pl.ds(0, 3)], S.at[pl.ds(0, 3)]), (stress.at[3], S.at[4]),
            (stress.at[4], S.at[3]), (stress.at[5], S.at[5]),
            (buoy, Bu), (lame1, L1), (lame2, L2),
        ])
    ]
    for c in loads:
        c.start()

    def zero_when_absent(flag, refs):
        @pl.when(jnp.logical_not(flag))
        def _():
            for r in refs:
                r[...] = jnp.zeros(r.shape, F32)

    zero_when_absent(has_b, [hb_s, hb_vx, hb_x, hb_xs])
    zero_when_absent(has_a, [ha_xx, ha_v, ha_x, ha_xs, lr])
    zero_when_absent(has_d, [hd_s, hd_vy, hd_c, hd_cs])
    zero_when_absent(has_u, [hu_yy, hu_v, hu_c, hu_cs])
    for r in (xf, xb, xsf, xsb, ls, tops):
        r[...] = jnp.zeros(r.shape, F32)

    barrier = pltpu.get_barrier_semaphore()
    for d in "fbud":
        dev, ok, _ = dirs[d]

        @pl.when(ok)
        def _():
            pl.semaphore_signal(barrier, inc=1, device_id=dev, device_id_type=MESH)

    pl.semaphore_wait(barrier, sum(f.astype(jnp.int32) for f in (has_b, has_a, has_d, has_u)))

    class Msg:
        def __init__(self, d, src, dst, ssem, rsem):
            dev, self.ok, self.inc = dirs[d]
            self.c = pltpu.make_async_remote_copy(
                src_ref=src, dst_ref=dst, send_sem=ssem, recv_sem=rsem,
                device_id=dev, device_id_type=MESH)

        def start(self):
            pl.when(self.ok)(lambda: self.c.start())

        def sent(self):
            pl.when(self.ok)(lambda: self.c.wait_send())

        def got(self):
            pl.when(self.inc)(lambda: self.c.wait_recv())

    count = [0]

    def msg(d, src, dst):
        i = count[0]
        count[0] += 1
        return Msg(d, src, dst, send.at[i], recv.at[i])

    size = zdim // PARTS
    am, bm = [], []
    for p in range(PARTS):
        zs = pl.ds(p * size, size)
        am.append([
            msg("f", S.at[pl.ds(3, 2), 1, zs], hb_s.at[:, zs]),
            msg("b", S.at[0, 0, zs], ha_xx.at[zs]),
            msg("u", S.at[pl.ds(4, 2), :, zs], hd_s.at[:, :, zs]),
            msg("d", S.at[1, :, zs], hu_yy.at[:, zs]),
        ])
        bm.append([
            msg("f", V.at[2, 1, zs], hb_vx.at[zs]),
            msg("b", V.at[pl.ds(0, 2), 0, zs], ha_v.at[:, zs]),
            msg("u", V.at[0, :, zs], hd_vy.at[:, zs]),
            msg("d", V.at[pl.ds(1, 2), :, zs], hu_v.at[:, :, zs]),
        ])
    csm = [msg("u", csu, hd_cs), msg("d", csd, hu_cs)]
    xsm = [msg("f", xsf, hb_xs), msg("b", xsb, ha_xs)]

    def xm(slot):
        return [
            Msg("f", xf.at[slot], hb_x.at[slot], xsend.at[0, slot], xrecv.at[0, slot]),
            Msg("b", xb.at[slot], ha_x.at[slot], xsend.at[1, slot], xrecv.at[1, slot]),
        ]

    def cm(slot):
        return [
            Msg("u", cu.at[slot], hd_c.at[slot], csend.at[0, slot], crecv.at[0, slot]),
            Msg("d", cd.at[slot], hu_c.at[slot], csend.at[1, slot], crecv.at[1, slot]),
        ]

    def lm(slot):
        return Msg("b", ls.at[slot], lr.at[slot], lsend.at[slot], lrecv.at[slot])

    lane = lax.broadcasted_iota(jnp.int32, (size, 128), 1)
    zrow = lax.broadcasted_iota(jnp.int32, (size, 128), 0)
    lane24 = lax.broadcasted_iota(jnp.int32, (24, 128), 1)
    lane8 = lax.broadcasted_iota(jnp.int32, (8, 128), 1)

    def ym(p, halo):
        return pltpu.roll(jnp.where(lane == 127, halo, p), 1, 1)

    def yp(p, halo):
        return pltpu.roll(jnp.where(lane == 0, halo, p), 127, 1)

    def zm(ref, c, x, z):
        if z == 0:
            return jnp.where(zrow == 0, 0.0, pltpu.roll(ref[c, x, 0:size, :], 1, 0))
        return pltpu.roll(ref[c, x, z - 8:z + size, :], 1, 0)[8:]

    def zp(ref, c, x, z):
        if z + size == zdim:
            return jnp.where(zrow == size - 1, 0.0, pltpu.roll(ref[c, x, z:zdim, :], size - 1, 0))
        return pltpu.roll(ref[c, x, z:z + size + 8, :], size + 7, 0)[:size]

    def rm(a):
        return pltpu.roll(a, 1, 0)

    def rp(a):
        return pltpu.roll(a, a.shape[0] - 1, 0)

    def cmn(a):
        return pltpu.roll(a, 1, 1)

    def cpl(a):
        return pltpu.roll(a, a.shape[1] - 1, 1)

    half = own // 2

    def fill_x(slot):
        for buf, rows in ((xf, slice(12, 16)), (xb, slice(0, 4))):
            buf[slot, 0:4, 0:own] = H[rows, 0:own]
            buf[slot, 4:8, 0:own] = M[rows, 0:own]
            buf[slot, 0:4, own:own + half] = N[rows, 0:half]
            buf[slot, 4:8, own:own + half] = N[rows, half:own]
        t = jnp.concatenate([V[1, 0, 0:1, :], V[1, 1, 0:1, :]], axis=0)
        xf[slot, 0:2, own + half:own + half + 128] = t
        tops[1:3, 0:128] = t

    def use_x(slot):
        at, left, right = slice(0, own), slice(0, half), slice(half, own)
        n = slice(own, own + half)
        a, b = ha_x, hb_x
        H[16:24, at] = jnp.concatenate([a[slot, 0:4, at], b[slot, 0:4, at]], axis=0)
        M[16:24, at] = jnp.concatenate([a[slot, 4:8, at], b[slot, 4:8, at]], axis=0)
        N[16:24, left] = jnp.concatenate([a[slot, 0:4, n], b[slot, 0:4, n]], axis=0)
        N[16:24, right] = jnp.concatenate([a[slot, 4:8, n], b[slot, 4:8, n]], axis=0)
        t = b[slot, 0:2, own + half:own + half + 128]
        tops[0:1, 0:128] = t[1:2, :]
        tops[3:4, 0:128] = t[0:1, :]

    def fill_c(slot):
        for i, r in enumerate((H, M, N)):
            cu[slot, 24 * i:24 * i + 24, :] = r[:, own - 128:own]
            cd[slot, 24 * i:24 * i + 24, :] = r[:, 0:128]
        cu[slot, 72:80, :] = tops[:, 0:128]
        cd[slot, 72:80, :] = tops[:, 0:128]

    def use_c(slot):
        for i, r in enumerate((H, M, N)):
            at = slice(24 * i, 24 * i + 24)
            r[:, own:lanes] = jnp.where(lane24 < 64, hu_c[slot, at, :], hd_c[slot, at, :])
        tops[:, 128:256] = jnp.where(
            lane8 < 8, hu_c[slot, 72:80, :], pltpu.roll(hd_c[slot, 72:80, :], 16, 1))

    def start_all(ms):
        for m in ms:
            m.start()

    for c in loads[7:11]:
        c.wait()
    for p in range(PARTS):
        start_all(am[p])
    for c in loads[:7]:
        c.wait()
    W[0:16, 0:own] = Wi[...].astype(F32)
    for buf, rows in ((xsf, slice(12, 16)), (xsb, slice(0, 4))):
        buf[0:4, 0:own] = W[rows, 0:own]
        buf[4:8, 0:own] = D[rows, 0:own]
    for q in range(own // 128):
        xsb[q:q + 1, own:own + 128] = W[4:5, 128 * q:128 * q + 128]
    fill_x(0)
    start_all(xm(0))
    start_all(xsm)
    for c in loads[11:]:
        c.wait()

    def bed_x():
        at = slice(0, own)
        W[16:24, at] = jnp.concatenate([ha_xs[0:4, at], hb_xs[0:4, at]], axis=0)
        D[16:24, at] = jnp.concatenate([ha_xs[4:8, at], hb_xs[4:8, at]], axis=0)
        w = W[:, at]
        Fx[:, at] = w * rp(w)
        nextw = jnp.concatenate(
            [ha_xs[q:q + 1, own:own + 128] for q in range(own // 128)], axis=1)
        Fx[16:20, at] = W[16:20, at] * jnp.concatenate([W[17:20, at], nextw], axis=0)
        for i, r in enumerate((W, D, Fx)):
            csu[24 * i:24 * i + 24, :] = r[:, own - 128:own]
            csd[24 * i:24 * i + 24, :] = r[:, 0:128]

    def ocean_setup():
        for i, r in enumerate((W, D, Fx)):
            at = slice(24 * i, 24 * i + 24)
            r[:, own:lanes] = jnp.where(lane24 < 64, hu_cs[at, :], hd_cs[at, :])
        w = W[...]
        d = D[...]
        fx = Fx[...]
        fy = w * cpl(w)
        wt[...] = WAVE_STEP * w
        Dx[...] = d + rp(d)
        Dy[...] = d + cpl(d)
        Bx[...] = VISCOSITY * fx
        By[...] = VISCOSITY * fy
        Ax[...] = fx * (1.0 - VISCOSITY * (rp(fx) + rm(fx) + cpl(fx) + cmn(fx)))
        Ay[...] = fy * (1.0 - VISCOSITY * (rp(fy) + rm(fy) + cpl(fy) + cmn(fy)))

    def mask_flow():
        fx = Fx[...]
        fy = W[...] * cpl(W[...])
        m, n = M[...], N[...]
        mm, nn = fx * m, fy * n
        dm, dn = m - mm, n - nn
        H[...] = H[...] - wt[...] * ((dm - rm(dm)) + (dn - cmn(dn)))
        M[...] = mm
        N[...] = nn

    first24, last24 = lane24 == 0, lane24 == 127

    def tile(r, q):
        q = q % nt
        return r[:, 128 * q:128 * q + 128]

    def from_left(a, left):
        return pltpu.roll(jnp.where(last24, left, a), 1, 1)

    def from_right(a, right):
        return pltpu.roll(jnp.where(first24, right, a), 127, 1)

    def substep(_, carry):
        m0, n0 = tile(M, 0), tile(N, 0)
        ml, nl = tile(M, nt - 1), tile(N, nt - 1)
        m, n = m0, n0

        def height(q, m, n, nl):
            mw, ns = rm(m), from_left(n, nl)
            return tile(H, q) - tile(wt, q) * ((m - mw) + (n - ns)), mw, ns

        h0, mw, ns = height(0, m, n, nl)
        h = h0
        for q in range(nt):
            at = slice(128 * q, 128 * q + 128)
            H[:, at] = h
            if q < nt - 1:
                mr, nr = tile(M, q + 1), tile(N, q + 1)
                hr, mwr, nsr = height(q + 1, mr, nr, n)
            else:
                mr, nr, hr, mwr, nsr = m0, n0, h0, None, None
            he, hn = rp(h), from_right(h, hr)
            M[:, at] = tile(Ax, q) * m + tile(Bx, q) * (
                ((rp(m) + mw) + (from_right(m, mr) + from_left(m, ml)))
                - (tile(Dx, q) + h + he) * (he - h))
            N[:, at] = tile(Ay, q) * n + tile(By, q) * (
                ((rp(n) + rm(n)) + (from_right(n, nr) + ns))
                - (tile(Dy, q) + h + hn) * (hn - h))
            ml, m, n, h, mw, ns = m, mr, nr, hr, mwr, nsr
        return carry

    er = lax.broadcasted_iota(jnp.int32, (128, 128), 0)
    ec = lax.broadcasted_iota(jnp.int32, (128, 128), 1)
    row24 = lax.broadcasted_iota(jnp.int32, (24, 128), 0)

    def spread_dot(a, ones):
        p0 = a.astype(jnp.bfloat16)
        r = a - p0.astype(F32)
        p1 = r.astype(jnp.bfloat16)
        p2 = (r - p1.astype(F32)).astype(jnp.bfloat16)
        e = ones.astype(jnp.bfloat16)
        return jnp.dot(jnp.concatenate([p0, p1, p2], axis=1),
                       jnp.concatenate([e, e, e], axis=0), preferred_element_type=F32)

    def lift():
        t = tops[:, 0:128]
        tiles = [t] + [pltpu.roll(t, 128 - 16 * q, 1) for q in range(1, nt - 1)]
        tiles.append(tops[:, 128:256])
        spread = jnp.where((ec // RATIO) == er, 1.0, 0.0)
        u = spread_dot(jnp.concatenate(tiles, axis=0), spread)
        for q in range(nt):
            r = u[8 * q:8 * q + 8, :]
            e = [jnp.broadcast_to(r[i:i + 1, :], (24, 128)) for i in range(4)]
            full = jnp.where(row24 < 8, e[0], jnp.where(row24 < 16, e[1], jnp.where(row24 < 20, e[2], e[3])))
            at = slice(128 * q, 128 * q + 128)
            H[:, at] = H[:, at] + UPLIFT_GAIN * W[:, at] * full

    def average(slot):
        p = W[0:16, 0:own] * H[0:16, 0:own]
        parts = [p[:, 128 * q:128 * q + 128] for q in range(nt - 1)]
        gather = jnp.where((er // RATIO) == ec, 1.0, 0.0)
        g = spread_dot(jnp.concatenate(parts, axis=0), gather)
        a0, a1 = g[0:8, :], g[8:16, :]
        for q in range(1, nt - 1):
            a0 = a0 + pltpu.roll(g[16 * q:16 * q + 8, :], 16 * q, 1)
            a1 = a1 + pltpu.roll(g[16 * q + 8:16 * q + 16, :], 16 * q, 1)
        scale = -LOAD_GAIN / (RATIO * RATIO)
        ls[slot, 0:1, :] = jnp.sum(a0, axis=0, keepdims=True) * scale
        ls[slot, 1:2, :] = jnp.sum(a1, axis=0, keepdims=True) * scale
        lm(slot).start()

    def apply_load(slot):
        lm(slot).got()
        S[2, 0, 0:1, :] = ls[slot, 1:2, :]
        S[2, 1, 0:1, :] = lr[slot, 0:1, :]

    def motion_part(z):
        zs = slice(z, z + size)
        for x in range(2):
            sb = SOLID_STEP * Bu[x, zs]
            xx, yy, zz, xz, xy, yz = (S[c, x, zs] for c in range(6))
            xx_a = S[0, 1, zs] if x == 0 else ha_xx[zs]
            xz_b = hb_s[0, zs] if x == 0 else S[3, 0, zs]
            xy_b = hb_s[1, zs] if x == 0 else S[4, 0, zs]
            V[2, x, zs] = V[2, x, zs] + sb * (
                (xx_a - xx) + (xy - ym(xy, hd_s[0, x, zs])) + (xz - zm(S, 3, x, z)))
            V[0, x, zs] = V[0, x, zs] + sb * (
                (xy - xy_b) + (yp(yy, hu_yy[x, zs]) - yy) + (yz - zm(S, 5, x, z)))
            V[1, x, zs] = V[1, x, zs] + sb * (
                (xz - xz_b) + (yz - ym(yz, hd_s[1, x, zs])) + (zp(S, 2, x, z) - zz))

    def stress_part(z):
        zs = slice(z, z + size)
        for x in range(2):
            vy, vz, vx = V[0, x, zs], V[1, x, zs], V[2, x, zs]
            vx_b = hb_vx[zs] if x == 0 else V[2, 0, zs]
            vy_a = V[0, 1, zs] if x == 0 else ha_v[0, zs]
            vz_a = V[1, 1, zs] if x == 0 else ha_v[1, zs]
            ex = vx - vx_b
            ey = vy - ym(vy, hd_vy[x, zs])
            ez = vz - zm(V, 1, x, z)
            l, g = SOLID_STEP * L1[x, zs], SOLID_STEP * L2[x, zs]
            tr = l * (ex + ey + ez)
            g2 = 2.0 * g
            S[0, x, zs] = S[0, x, zs] + (tr + g2 * ex)
            S[1, x, zs] = S[1, x, zs] + (tr + g2 * ey)
            S[2, x, zs] = S[2, x, zs] + (tr + g2 * ez)
            S[3, x, zs] = S[3, x, zs] + g * ((zp(V, 2, x, z) - vx) + (vz_a - vz))
            S[4, x, zs] = S[4, x, zs] + g * ((yp(vx, hu_v[1, x, zs]) - vx) + (vy_a - vy))
            S[5, x, zs] = S[5, x, zs] + g * ((zp(V, 0, x, z) - vy) + (yp(vz, hu_v[0, x, zs]) - vz))

    def step(k, carry):
        slot = lax.rem(k, 2)
        nslot = lax.rem(k + 1, 2)

        xms = xm(slot)
        cms = cm(slot)
        for m in xms:
            m.got()
        use_x(slot)

        @pl.when(k == 0)
        def _():
            for m in xsm:
                m.got()
            bed_x()
            start_all(csm)

        fill_c(slot)
        start_all(cms)

        for p in range(PARTS):
            for m in am[p]:
                m.got()
            if p == 0:
                @pl.when(k > 0)
                def _():
                    apply_load(nslot)

            motion_part(p * size)
            start_all(bm[p])

        for m in cms:
            m.got()
        use_c(slot)

        @pl.when(k == 0)
        def _():
            for m in csm:
                m.got()
            ocean_setup()
            mask_flow()

        lift()
        lax.fori_loop(0, NSUB, substep, 0)
        last = k == STEPS - 1
        pl.when(last)(lambda: average(slot))

        @pl.when(k < STEPS - 1)
        def _():
            fill_x(nslot)
            start_all(xm(nslot))

        for p in range(PARTS):
            for m in bm[p]:
                m.got()
            for m in am[p]:
                m.sent()
            stress_part(p * size)

            @pl.when(k < STEPS - 1)
            def _():
                start_all(am[p])

        pl.when(jnp.logical_not(last))(lambda: average(slot))
        for ms in bm:
            for m in ms:
                m.sent()
        for m in xms + cms:
            m.sent()
        lm(slot).sent()
        return carry

    lax.fori_loop(0, STEPS, step, 0)
    for m in xsm + csm:
        m.sent()
    apply_load((STEPS - 1) % 2)


def write_out(V, S, H, M, N, o_motion, o_stress, o_surf, o_mom, sem):
    rows, own = o_surf.shape
    at = (pl.ds(0, rows), pl.ds(0, own))
    outs = [
        pltpu.make_async_copy(a, b, sem.at[i])
        for i, (a, b) in enumerate([
            (S.at[pl.ds(0, 3)], o_stress.at[pl.ds(0, 3)]),
            (V.at[pl.ds(0, 2)], o_motion.at[pl.ds(1, 2)]), (V.at[2], o_motion.at[0]),
            (S.at[4], o_stress.at[3]), (S.at[3], o_stress.at[4]), (S.at[5], o_stress.at[5]),
            (H.at[at], o_surf), (M.at[at], o_mom.at[0]), (N.at[at], o_mom.at[1]),
        ])
    ]
    for c in outs:
        c.start()
    for c in outs:
        c.wait()


def body(nx, ny, motion, stress, buoyancy, lame_first, lame_shear, surface, momentum, bathymetry, wet_mask):
    plane = motion.shape[2:]
    two = motion.shape[1:]
    ext = (24, surface.shape[1] + 128)

    def v(*shape):
        return pltpu.VMEM(shape, F32)

    scratch = [v(*two)] * 3 + [pltpu.VMEM(wet_mask.shape, jnp.int32)] + [v(*ext)] * 10
    scratch += [v(2, *plane), v(*plane), v(2, *two), v(*two)]
    scratch += [v(*plane), v(2, *plane), v(*two), v(2, *two)]
    scratch += [v(2, 80, 128)] * 4 + [v(72, 128)] * 4
    wide = surface.shape[1]
    scratch += [v(2, 8, wide + wide // 2 + 128)] * 4 + [v(8, wide + 128)] * 4
    scratch += [v(2, 8, 128), v(2, 8, 128), v(8, 256)]
    dma = pltpu.SemaphoreType.DMA
    scratch += [dma((14,)), dma((8 * PARTS + 4,)), dma((8 * PARTS + 4,)), dma((2, 2)), dma((2, 2)), dma((2, 2)), dma((2, 2)), dma((2,)), dma((2,))]
    state = [motion.shape, stress.shape, ext, ext, ext]
    hbm = pl.BlockSpec(memory_space=pltpu.HBM)
    held = pl.pallas_call(
        functools.partial(kernel, nx, ny),
        out_shape=[pltpu.VMEM(shape, F32) for shape in state],
        in_specs=[hbm] * 9,
        out_specs=[pl.BlockSpec(memory_space=pltpu.VMEM)] * 5,
        scratch_shapes=scratch,
        compiler_params=pltpu.CompilerParams(
            collective_id=0, has_side_effects=True, vmem_limit_bytes=56 * 1024 * 1024
        ),
        name="coupled",
    )(motion, stress, buoyancy, lame_first, lame_shear, surface, momentum, bathymetry, wet_mask)
    return pl.pallas_call(
        write_out,
        out_shape=[
            jax.ShapeDtypeStruct(a.shape, F32) for a in (motion, stress, surface, momentum)
        ],
        in_specs=[pl.BlockSpec(memory_space=pl.ANY)] * 5,
        out_specs=[pl.BlockSpec(memory_space=pl.ANY)] * 4,
        scratch_shapes=[dma((9,))],
        compiler_params=pltpu.CompilerParams(vmem_limit_bytes=1024 * 1024),
        name="write_out",
    )(*held)


def solution(mesh):
    return jax.shard_map(
        functools.partial(body, mesh.shape["gx"], mesh.shape["gy"]),
        mesh=mesh,
        in_specs=(
            P(None, "gx", None, "gy"),
            P(None, "gx", None, "gy"),
            P("gx", None, "gy"),
            P("gx", None, "gy"),
            P("gx", None, "gy"),
            P("gx", "gy"),
            P(None, "gx", "gy"),
            P("gx", "gy"),
            P("gx", "gy"),
        ),
        out_specs=(
            P(None, "gx", None, "gy"),
            P(None, "gx", None, "gy"),
            P("gx", "gy"),
            P(None, "gx", "gy"),
        ),
        check_vma=False,
    )
```

```python
import functools

import jax
import jax.numpy as jnp
from jax import lax
from jax.experimental import pallas as pl
from jax.experimental.pallas import tpu as pltpu
from jax.sharding import PartitionSpec as P

RATIO = 8
STEPS = 4
NSUB = 4
PARTS = 3
SOLID_STEP = 0.2
WAVE_STEP = 0.1
VISCOSITY = 0.05
UPLIFT_GAIN = 0.25
LOAD_GAIN = 8.0

MESH = pl.DeviceIdType.MESH
F32 = jnp.float32


def kernel(
    nx, ny,
    motion, stress, buoy, lame1, lame2, surf, mom, bath, wetm,
    V, S, H, M, N,
    Bu, L1, L2, Wi, W, D, wt, Dx, Dy, Ax, Bx, Ay, By, Fx,
    hb_s, ha_xx, hd_s, hu_yy,
    hb_vx, ha_v, hd_vy, hu_v,
    cu, cd, hd_c, hu_c, csu, csd, hd_cs, hu_cs,
    xf, xb, hb_x, ha_x, xsf, xsb, hb_xs, ha_xs,
    ls, lr, tops,
    in_sem, send, recv, csend, crecv, xsend, xrecv, lsend, lrecv,
):
    gx = lax.axis_index("gx")
    gy = lax.axis_index("gy")
    has_b, has_a, has_d, has_u = gx > 0, gx < nx - 1, gy > 0, gy < ny - 1
    ahead = (jnp.minimum(gx + 1, nx - 1), gy)
    behind = (jnp.maximum(gx - 1, 0), gy)
    up = (gx, jnp.minimum(gy + 1, ny - 1))
    down = (gx, jnp.maximum(gy - 1, 0))
    dirs = {
        "f": (ahead, has_a, has_b),
        "b": (behind, has_b, has_a),
        "u": (up, has_u, has_d),
        "d": (down, has_d, has_u),
    }
    zdim = S.shape[2]
    lanes = H.shape[1]
    own = surf.shape[1]
    nt = lanes // 128

    loads = [
        pltpu.make_async_copy(a, b, in_sem.at[i])
        for i, (a, b) in enumerate([
            (stress.at[pl.ds(0, 3)], S.at[pl.ds(0, 3)]), (stress.at[3], S.at[4]),
            (stress.at[4], S.at[3]), (stress.at[5], S.at[5]),
            (wetm, Wi),
            (bath, D.at[pl.ds(0, 16), pl.ds(0, own)]),
            (surf, H.at[pl.ds(0, 16), pl.ds(0, own)]),
            (mom.at[0], M.at[pl.ds(0, 16), pl.ds(0, own)]),
            (mom.at[1], N.at[pl.ds(0, 16), pl.ds(0, own)]),
            (motion.at[pl.ds(1, 2)], V.at[pl.ds(0, 2)]), (motion.at[0], V.at[2]),
            (buoy, Bu), (lame1, L1), (lame2, L2),
        ])
    ]
    for c in loads:
        c.start()

    def zero_when_absent(flag, refs):
        @pl.when(jnp.logical_not(flag))
        def _():
            for r in refs:
                r[...] = jnp.zeros(r.shape, F32)

    zero_when_absent(has_b, [hb_s, hb_vx, hb_x, hb_xs])
    zero_when_absent(has_a, [ha_xx, ha_v, ha_x, ha_xs, lr])
    zero_when_absent(has_d, [hd_s, hd_vy, hd_c, hd_cs])
    zero_when_absent(has_u, [hu_yy, hu_v, hu_c, hu_cs])
    for r in (xf, xb, xsf, xsb, ls, tops):
        r[...] = jnp.zeros(r.shape, F32)

    barrier = pltpu.get_barrier_semaphore()
    for d in "fbud":
        dev, ok, _ = dirs[d]

        @pl.when(ok)
        def _():
            pl.semaphore_signal(barrier, inc=1, device_id=dev, device_id_type=MESH)

    pl.semaphore_wait(barrier, sum(f.astype(jnp.int32) for f in (has_b, has_a, has_d, has_u)))

    class Msg:
        def __init__(self, d, src, dst, ssem, rsem):
            dev, self.ok, self.inc = dirs[d]
            self.c = pltpu.make_async_remote_copy(
                src_ref=src, dst_ref=dst, send_sem=ssem, recv_sem=rsem,
                device_id=dev, device_id_type=MESH)

        def start(self):
            pl.when(self.ok)(lambda: self.c.start())

        def sent(self):
            pl.when(self.ok)(lambda: self.c.wait_send())

        def got(self):
            pl.when(self.inc)(lambda: self.c.wait_recv())

    count = [0]

    def msg(d, src, dst):
        i = count[0]
        count[0] += 1
        return Msg(d, src, dst, send.at[i], recv.at[i])

    size = zdim // PARTS
    am, bm = [], []
    for p in range(PARTS):
        zs = pl.ds(p * size, size)
        am.append([
            msg("f", S.at[pl.ds(3, 2), 1, zs], hb_s.at[:, zs]),
            msg("b", S.at[0, 0, zs], ha_xx.at[zs]),
            msg("u", S.at[pl.ds(4, 2), :, zs], hd_s.at[:, :, zs]),
            msg("d", S.at[1, :, zs], hu_yy.at[:, zs]),
        ])
        bm.append([
            msg("f", V.at[2, 1, zs], hb_vx.at[zs]),
            msg("b", V.at[pl.ds(0, 2), 0, zs], ha_v.at[:, zs]),
            msg("u", V.at[0, :, zs], hd_vy.at[:, zs]),
            msg("d", V.at[pl.ds(1, 2), :, zs], hu_v.at[:, :, zs]),
        ])
    csm = [msg("u", csu, hd_cs), msg("d", csd, hu_cs)]
    xsm = [msg("f", xsf, hb_xs), msg("b", xsb, ha_xs)]

    def xm(slot):
        return [
            Msg("f", xf.at[slot], hb_x.at[slot], xsend.at[0, slot], xrecv.at[0, slot]),
            Msg("b", xb.at[slot], ha_x.at[slot], xsend.at[1, slot], xrecv.at[1, slot]),
        ]

    def cm(slot):
        return [
            Msg("u", cu.at[slot], hd_c.at[slot], csend.at[0, slot], crecv.at[0, slot]),
            Msg("d", cd.at[slot], hu_c.at[slot], csend.at[1, slot], crecv.at[1, slot]),
        ]

    def lm(slot):
        return Msg("b", ls.at[slot], lr.at[slot], lsend.at[slot], lrecv.at[slot])

    lane = lax.broadcasted_iota(jnp.int32, (size, 128), 1)
    zrow = lax.broadcasted_iota(jnp.int32, (size, 128), 0)
    lane24 = lax.broadcasted_iota(jnp.int32, (24, 128), 1)
    lane8 = lax.broadcasted_iota(jnp.int32, (8, 128), 1)

    def ym(p, halo):
        return pltpu.roll(jnp.where(lane == 127, halo, p), 1, 1)

    def yp(p, halo):
        return pltpu.roll(jnp.where(lane == 0, halo, p), 127, 1)

    def zm(ref, c, x, z):
        if z == 0:
            return jnp.where(zrow == 0, 0.0, pltpu.roll(ref[c, x, 0:size, :], 1, 0))
        return pltpu.roll(ref[c, x, z - 8:z + size, :], 1, 0)[8:]

    def zp(ref, c, x, z):
        if z + size == zdim:
            return jnp.where(zrow == size - 1, 0.0, pltpu.roll(ref[c, x, z:zdim, :], size - 1, 0))
        return pltpu.roll(ref[c, x, z:z + size + 8, :], size + 7, 0)[:size]

    def rm(a):
        return pltpu.roll(a, 1, 0)

    def rp(a):
        return pltpu.roll(a, a.shape[0] - 1, 0)

    def cmn(a):
        return pltpu.roll(a, 1, 1)

    def cpl(a):
        return pltpu.roll(a, a.shape[1] - 1, 1)

    half = own // 2

    def fill_x(slot):
        for buf, rows in ((xf, slice(12, 16)), (xb, slice(0, 4))):
            buf[slot, 0:4, 0:own] = H[rows, 0:own]
            buf[slot, 4:8, 0:own] = M[rows, 0:own]
            buf[slot, 0:4, own:own + half] = N[rows, 0:half]
            buf[slot, 4:8, own:own + half] = N[rows, half:own]
        t = jnp.concatenate([V[1, 0, 0:1, :], V[1, 1, 0:1, :]], axis=0)
        xf[slot, 0:2, own + half:own + half + 128] = t
        tops[1:3, 0:128] = t

    def use_x(slot):
        at, left, right = slice(0, own), slice(0, half), slice(half, own)
        n = slice(own, own + half)
        a, b = ha_x, hb_x
        H[16:24, at] = jnp.concatenate([a[slot, 0:4, at], b[slot, 0:4, at]], axis=0)
        M[16:24, at] = jnp.concatenate([a[slot, 4:8, at], b[slot, 4:8, at]], axis=0)
        N[16:24, left] = jnp.concatenate([a[slot, 0:4, n], b[slot, 0:4, n]], axis=0)
        N[16:24, right] = jnp.concatenate([a[slot, 4:8, n], b[slot, 4:8, n]], axis=0)
        t = b[slot, 0:2, own + half:own + half + 128]
        tops[0:1, 0:128] = t[1:2, :]
        tops[3:4, 0:128] = t[0:1, :]

    def fill_c(slot):
        for i, r in enumerate((H, M, N)):
            cu[slot, 24 * i:24 * i + 24, :] = r[:, own - 128:own]
            cd[slot, 24 * i:24 * i + 24, :] = r[:, 0:128]
        cu[slot, 72:80, :] = tops[:, 0:128]
        cd[slot, 72:80, :] = tops[:, 0:128]

    def use_c(slot):
        for i, r in enumerate((H, M, N)):
            at = slice(24 * i, 24 * i + 24)
            r[:, own:lanes] = jnp.where(lane24 < 64, hu_c[slot, at, :], hd_c[slot, at, :])
        tops[:, 128:256] = jnp.where(
            lane8 < 8, hu_c[slot, 72:80, :], pltpu.roll(hd_c[slot, 72:80, :], 16, 1))

    def start_all(ms):
        for m in ms:
            m.start()

    for c in loads[:4]:
        c.wait()
    for p in range(PARTS):
        start_all(am[p])
    for c in loads[4:11]:
        c.wait()
    W[0:16, 0:own] = Wi[...].astype(F32)
    for buf, rows in ((xsf, slice(12, 16)), (xsb, slice(0, 4))):
        buf[0:4, 0:own] = W[rows, 0:own]
        buf[4:8, 0:own] = D[rows, 0:own]
    for q in range(own // 128):
        xsb[q:q + 1, own:own + 128] = W[4:5, 128 * q:128 * q + 128]
    fill_x(0)
    start_all(xm(0))
    start_all(xsm)
    for c in loads[11:]:
        c.wait()

    def bed_x():
        at = slice(0, own)
        W[16:24, at] = jnp.concatenate([ha_xs[0:4, at], hb_xs[0:4, at]], axis=0)
        D[16:24, at] = jnp.concatenate([ha_xs[4:8, at], hb_xs[4:8, at]], axis=0)
        w = W[:, at]
        Fx[:, at] = w * rp(w)
        nextw = jnp.concatenate(
            [ha_xs[q:q + 1, own:own + 128] for q in range(own // 128)], axis=1)
        Fx[16:20, at] = W[16:20, at] * jnp.concatenate([W[17:20, at], nextw], axis=0)
        for i, r in enumerate((W, D, Fx)):
            csu[24 * i:24 * i + 24, :] = r[:, own - 128:own]
            csd[24 * i:24 * i + 24, :] = r[:, 0:128]

    def ocean_setup():
        for i, r in enumerate((W, D, Fx)):
            at = slice(24 * i, 24 * i + 24)
            r[:, own:lanes] = jnp.where(lane24 < 64, hu_cs[at, :], hd_cs[at, :])
        w = W[...]
        d = D[...]
        fx = Fx[...]
        fy = w * cpl(w)
        wt[...] = WAVE_STEP * w
        Dx[...] = d + rp(d)
        Dy[...] = d + cpl(d)
        Bx[...] = VISCOSITY * fx
        By[...] = VISCOSITY * fy
        Ax[...] = fx * (1.0 - VISCOSITY * (rp(fx) + rm(fx) + cpl(fx) + cmn(fx)))
        Ay[...] = fy * (1.0 - VISCOSITY * (rp(fy) + rm(fy) + cpl(fy) + cmn(fy)))

    def mask_flow():
        fx = Fx[...]
        fy = W[...] * cpl(W[...])
        m, n = M[...], N[...]
        mm, nn = fx * m, fy * n
        dm, dn = m - mm, n - nn
        H[...] = H[...] - wt[...] * ((dm - rm(dm)) + (dn - cmn(dn)))
        M[...] = mm
        N[...] = nn

    first24, last24 = lane24 == 0, lane24 == 127

    def tile(r, q):
        q = q % nt
        return r[:, 128 * q:128 * q + 128]

    def from_left(a, left):
        return pltpu.roll(jnp.where(last24, left, a), 1, 1)

    def from_right(a, right):
        return pltpu.roll(jnp.where(first24, right, a), 127, 1)

    def substep(_, carry):
        m0, n0 = tile(M, 0), tile(N, 0)
        ml, nl = tile(M, nt - 1), tile(N, nt - 1)
        m, n = m0, n0

        def height(q, m, n, nl):
            mw, ns = rm(m), from_left(n, nl)
            return tile(H, q) - tile(wt, q) * ((m - mw) + (n - ns)), mw, ns

        h0, mw, ns = height(0, m, n, nl)
        h = h0
        for q in range(nt):
            at = slice(128 * q, 128 * q + 128)
            H[:, at] = h
            if q < nt - 1:
                mr, nr = tile(M, q + 1), tile(N, q + 1)
                hr, mwr, nsr = height(q + 1, mr, nr, n)
            else:
                mr, nr, hr, mwr, nsr = m0, n0, h0, None, None
            he, hn = rp(h), from_right(h, hr)
            M[:, at] = tile(Ax, q) * m + tile(Bx, q) * (
                ((rp(m) + mw) + (from_right(m, mr) + from_left(m, ml)))
                - (tile(Dx, q) + h + he) * (he - h))
            N[:, at] = tile(Ay, q) * n + tile(By, q) * (
                ((rp(n) + rm(n)) + (from_right(n, nr) + ns))
                - (tile(Dy, q) + h + hn) * (hn - h))
            ml, m, n, h, mw, ns = m, mr, nr, hr, mwr, nsr
        return carry

    er = lax.broadcasted_iota(jnp.int32, (128, 128), 0)
    ec = lax.broadcasted_iota(jnp.int32, (128, 128), 1)
    row24 = lax.broadcasted_iota(jnp.int32, (24, 128), 0)

    def spread_dot(a, ones):
        p0 = a.astype(jnp.bfloat16)
        r = a - p0.astype(F32)
        p1 = r.astype(jnp.bfloat16)
        p2 = (r - p1.astype(F32)).astype(jnp.bfloat16)
        e = ones.astype(jnp.bfloat16)
        return jnp.dot(jnp.concatenate([p0, p1, p2], axis=1),
                       jnp.concatenate([e, e, e], axis=0), preferred_element_type=F32)

    def lift():
        t = tops[:, 0:128]
        tiles = [t] + [pltpu.roll(t, 128 - 16 * q, 1) for q in range(1, nt - 1)]
        tiles.append(tops[:, 128:256])
        spread = jnp.where((ec // RATIO) == er, 1.0, 0.0)
        u = spread_dot(jnp.concatenate(tiles, axis=0), spread)
        for q in range(nt):
            r = u[8 * q:8 * q + 8, :]
            e = [jnp.broadcast_to(r[i:i + 1, :], (24, 128)) for i in range(4)]
            full = jnp.where(row24 < 8, e[0], jnp.where(row24 < 16, e[1], jnp.where(row24 < 20, e[2], e[3])))
            at = slice(128 * q, 128 * q + 128)
            H[:, at] = H[:, at] + UPLIFT_GAIN * W[:, at] * full

    def average(slot):
        p = W[0:16, 0:own] * H[0:16, 0:own]
        parts = [p[:, 128 * q:128 * q + 128] for q in range(nt - 1)]
        gather = jnp.where((er // RATIO) == ec, 1.0, 0.0)
        g = spread_dot(jnp.concatenate(parts, axis=0), gather)
        a0, a1 = g[0:8, :], g[8:16, :]
        for q in range(1, nt - 1):
            a0 = a0 + pltpu.roll(g[16 * q:16 * q + 8, :], 16 * q, 1)
            a1 = a1 + pltpu.roll(g[16 * q + 8:16 * q + 16, :], 16 * q, 1)
        scale = -LOAD_GAIN / (RATIO * RATIO)
        ls[slot, 0:1, :] = jnp.sum(a0, axis=0, keepdims=True) * scale
        ls[slot, 1:2, :] = jnp.sum(a1, axis=0, keepdims=True) * scale
        lm(slot).start()

    def apply_load(slot):
        lm(slot).got()
        S[2, 0, 0:1, :] = ls[slot, 1:2, :]
        S[2, 1, 0:1, :] = lr[slot, 0:1, :]

    def motion_part(z):
        zs = slice(z, z + size)
        for x in range(2):
            sb = SOLID_STEP * Bu[x, zs]
            xx, yy, zz, xz, xy, yz = (S[c, x, zs] for c in range(6))
            xx_a = S[0, 1, zs] if x == 0 else ha_xx[zs]
            xz_b = hb_s[0, zs] if x == 0 else S[3, 0, zs]
            xy_b = hb_s[1, zs] if x == 0 else S[4, 0, zs]
            V[2, x, zs] = V[2, x, zs] + sb * (
                (xx_a - xx) + (xy - ym(xy, hd_s[0, x, zs])) + (xz - zm(S, 3, x, z)))
            V[0, x, zs] = V[0, x, zs] + sb * (
                (xy - xy_b) + (yp(yy, hu_yy[x, zs]) - yy) + (yz - zm(S, 5, x, z)))
            V[1, x, zs] = V[1, x, zs] + sb * (
                (xz - xz_b) + (yz - ym(yz, hd_s[1, x, zs])) + (zp(S, 2, x, z) - zz))

    def stress_part(z):
        zs = slice(z, z + size)
        for x in range(2):
            vy, vz, vx = V[0, x, zs], V[1, x, zs], V[2, x, zs]
            vx_b = hb_vx[zs] if x == 0 else V[2, 0, zs]
            vy_a = V[0, 1, zs] if x == 0 else ha_v[0, zs]
            vz_a = V[1, 1, zs] if x == 0 else ha_v[1, zs]
            ex = vx - vx_b
            ey = vy - ym(vy, hd_vy[x, zs])
            ez = vz - zm(V, 1, x, z)
            l, g = SOLID_STEP * L1[x, zs], SOLID_STEP * L2[x, zs]
            tr = l * (ex + ey + ez)
            g2 = 2.0 * g
            S[0, x, zs] = S[0, x, zs] + (tr + g2 * ex)
            S[1, x, zs] = S[1, x, zs] + (tr + g2 * ey)
            S[2, x, zs] = S[2, x, zs] + (tr + g2 * ez)
            S[3, x, zs] = S[3, x, zs] + g * ((zp(V, 2, x, z) - vx) + (vz_a - vz))
            S[4, x, zs] = S[4, x, zs] + g * ((yp(vx, hu_v[1, x, zs]) - vx) + (vy_a - vy))
            S[5, x, zs] = S[5, x, zs] + g * ((zp(V, 0, x, z) - vy) + (yp(vz, hu_v[0, x, zs]) - vz))

    def step(k, carry):
        slot = lax.rem(k, 2)
        nslot = lax.rem(k + 1, 2)

        xms = xm(slot)
        cms = cm(slot)
        for m in xms:
            m.got()
        use_x(slot)

        @pl.when(k == 0)
        def _():
            for m in xsm:
                m.got()
            bed_x()
            start_all(csm)

        fill_c(slot)
        start_all(cms)

        for p in range(PARTS):
            for m in am[p]:
                m.got()
            if p == 0:
                @pl.when(k > 0)
                def _():
                    apply_load(nslot)

            motion_part(p * size)
            start_all(bm[p])

        for m in cms:
            m.got()
        use_c(slot)

        @pl.when(k == 0)
        def _():
            for m in csm:
                m.got()
            ocean_setup()
            mask_flow()

        lift()
        lax.fori_loop(0, NSUB, substep, 0)
        last = k == STEPS - 1
        pl.when(last)(lambda: average(slot))

        @pl.when(k < STEPS - 1)
        def _():
            fill_x(nslot)
            start_all(xm(nslot))

        for p in range(PARTS):
            for m in bm[p]:
                m.got()
            for m in am[p]:
                m.sent()
            stress_part(p * size)

            @pl.when(k < STEPS - 1)
            def _():
                start_all(am[p])

        pl.when(jnp.logical_not(last))(lambda: average(slot))
        for ms in bm:
            for m in ms:
                m.sent()
        for m in xms + cms:
            m.sent()
        lm(slot).sent()
        return carry

    lax.fori_loop(0, STEPS, step, 0)
    for m in xsm + csm:
        m.sent()
    apply_load((STEPS - 1) % 2)


def write_out(V, S, H, M, N, o_motion, o_stress, o_surf, o_mom, sem):
    rows, own = o_surf.shape
    at = (pl.ds(0, rows), pl.ds(0, own))
    outs = [
        pltpu.make_async_copy(a, b, sem.at[i])
        for i, (a, b) in enumerate([
            (S.at[pl.ds(0, 3)], o_stress.at[pl.ds(0, 3)]),
            (V.at[pl.ds(0, 2)], o_motion.at[pl.ds(1, 2)]), (V.at[2], o_motion.at[0]),
            (S.at[4], o_stress.at[3]), (S.at[3], o_stress.at[4]), (S.at[5], o_stress.at[5]),
            (H.at[at], o_surf), (M.at[at], o_mom.at[0]), (N.at[at], o_mom.at[1]),
        ])
    ]
    for c in outs:
        c.start()
    for c in outs:
        c.wait()


def body(nx, ny, motion, stress, buoyancy, lame_first, lame_shear, surface, momentum, bathymetry, wet_mask):
    plane = motion.shape[2:]
    two = motion.shape[1:]
    ext = (24, surface.shape[1] + 128)

    def v(*shape):
        return pltpu.VMEM(shape, F32)

    scratch = [v(*two)] * 3 + [pltpu.VMEM(wet_mask.shape, jnp.int32)] + [v(*ext)] * 10
    scratch += [v(2, *plane), v(*plane), v(2, *two), v(*two)]
    scratch += [v(*plane), v(2, *plane), v(*two), v(2, *two)]
    scratch += [v(2, 80, 128)] * 4 + [v(72, 128)] * 4
    wide = surface.shape[1]
    scratch += [v(2, 8, wide + wide // 2 + 128)] * 4 + [v(8, wide + 128)] * 4
    scratch += [v(2, 8, 128), v(2, 8, 128), v(8, 256)]
    dma = pltpu.SemaphoreType.DMA
    scratch += [dma((14,)), dma((8 * PARTS + 4,)), dma((8 * PARTS + 4,)), dma((2, 2)), dma((2, 2)), dma((2, 2)), dma((2, 2)), dma((2,)), dma((2,))]
    state = [motion.shape, stress.shape, ext, ext, ext]
    hbm = pl.BlockSpec(memory_space=pltpu.HBM)
    held = pl.pallas_call(
        functools.partial(kernel, nx, ny),
        out_shape=[pltpu.VMEM(shape, F32) for shape in state],
        in_specs=[hbm] * 9,
        out_specs=[pl.BlockSpec(memory_space=pltpu.VMEM)] * 5,
        scratch_shapes=scratch,
        compiler_params=pltpu.CompilerParams(
            collective_id=0, has_side_effects=True, vmem_limit_bytes=56 * 1024 * 1024
        ),
        name="coupled",
    )(motion, stress, buoyancy, lame_first, lame_shear, surface, momentum, bathymetry, wet_mask)
    return pl.pallas_call(
        write_out,
        out_shape=[
            jax.ShapeDtypeStruct(a.shape, F32) for a in (motion, stress, surface, momentum)
        ],
        in_specs=[pl.BlockSpec(memory_space=pl.ANY)] * 5,
        out_specs=[pl.BlockSpec(memory_space=pl.ANY)] * 4,
        scratch_shapes=[dma((9,))],
        compiler_params=pltpu.CompilerParams(vmem_limit_bytes=1024 * 1024),
        name="write_out",
    )(*held)


def solution(mesh):
    return jax.shard_map(
        functools.partial(body, mesh.shape["gx"], mesh.shape["gy"]),
        mesh=mesh,
        in_specs=(
            P(None, "gx", None, "gy"),
            P(None, "gx", None, "gy"),
            P("gx", None, "gy"),
            P("gx", None, "gy"),
            P("gx", None, "gy"),
            P("gx", "gy"),
            P(None, "gx", "gy"),
            P("gx", "gy"),
            P("gx", "gy"),
        ),
        out_specs=(
            P(None, "gx", None, "gy"),
            P(None, "gx", None, "gy"),
            P("gx", "gy"),
            P(None, "gx", "gy"),
        ),
        check_vma=False,
    )
```

```python
import functools

import jax
import jax.numpy as jnp
from jax import lax
from jax.experimental import pallas as pl
from jax.experimental.pallas import tpu as pltpu
from jax.sharding import PartitionSpec as P

RATIO = 8
STEPS = 4
NSUB = 4
PARTS = 2
SOLID_STEP = 0.2
WAVE_STEP = 0.1
VISCOSITY = 0.05
UPLIFT_GAIN = 0.25
LOAD_GAIN = 8.0

MESH = pl.DeviceIdType.MESH
F32 = jnp.float32


def kernel(
    nx, ny,
    motion, stress, buoy, lame1, lame2, surf, mom, bath, wetm,
    V, S, H, M, N,
    Bu, L1, L2, Wi, W, D, wt, Dx, Dy, Ax, Bx, Ay, By, Fx,
    hb_s, ha_xx, hd_s, hu_yy,
    hb_vx, ha_v, hd_vy, hu_v,
    cu, cd, hd_c, hu_c, csu, csd, hd_cs, hu_cs,
    xf, xb, hb_x, ha_x, xsf, xsb, hb_xs, ha_xs,
    ls, lr, tops,
    in_sem, send, recv, csend, crecv, xsend, xrecv, lsend, lrecv,
):
    gx = lax.axis_index("gx")
    gy = lax.axis_index("gy")
    has_b, has_a, has_d, has_u = gx > 0, gx < nx - 1, gy > 0, gy < ny - 1
    ahead = (jnp.minimum(gx + 1, nx - 1), gy)
    behind = (jnp.maximum(gx - 1, 0), gy)
    up = (gx, jnp.minimum(gy + 1, ny - 1))
    down = (gx, jnp.maximum(gy - 1, 0))
    dirs = {
        "f": (ahead, has_a, has_b),
        "b": (behind, has_b, has_a),
        "u": (up, has_u, has_d),
        "d": (down, has_d, has_u),
    }
    zdim = S.shape[2]
    lanes = H.shape[1]
    own = surf.shape[1]
    nt = lanes // 128

    loads = [
        pltpu.make_async_copy(a, b, in_sem.at[i])
        for i, (a, b) in enumerate([
            (stress.at[pl.ds(0, 3)], S.at[pl.ds(0, 3)]), (stress.at[3], S.at[4]),
            (stress.at[4], S.at[3]), (stress.at[5], S.at[5]),
            (wetm, Wi),
            (bath, D.at[pl.ds(0, 16), pl.ds(0, own)]),
            (surf, H.at[pl.ds(0, 16), pl.ds(0, own)]),
            (mom.at[0], M.at[pl.ds(0, 16), pl.ds(0, own)]),
            (mom.at[1], N.at[pl.ds(0, 16), pl.ds(0, own)]),
            (motion.at[pl.ds(1, 2)], V.at[pl.ds(0, 2)]), (motion.at[0], V.at[2]),
            (buoy, Bu), (lame1, L1), (lame2, L2),
        ])
    ]
    for c in loads:
        c.start()

    def zero_when_absent(flag, refs):
        @pl.when(jnp.logical_not(flag))
        def _():
            for r in refs:
                r[...] = jnp.zeros(r.shape, F32)

    zero_when_absent(has_b, [hb_s, hb_vx, hb_x, hb_xs])
    zero_when_absent(has_a, [ha_xx, ha_v, ha_x, ha_xs, lr])
    zero_when_absent(has_d, [hd_s, hd_vy, hd_c, hd_cs])
    zero_when_absent(has_u, [hu_yy, hu_v, hu_c, hu_cs])
    for r in (xf, xb, xsf, xsb, ls, tops):
        r[...] = jnp.zeros(r.shape, F32)

    barrier = pltpu.get_barrier_semaphore()
    for d in "fbud":
        dev, ok, _ = dirs[d]

        @pl.when(ok)
        def _():
            pl.semaphore_signal(barrier, inc=1, device_id=dev, device_id_type=MESH)

    pl.semaphore_wait(barrier, sum(f.astype(jnp.int32) for f in (has_b, has_a, has_d, has_u)))

    class Msg:
        def __init__(self, d, src, dst, ssem, rsem):
            dev, self.ok, self.inc = dirs[d]
            self.c = pltpu.make_async_remote_copy(
                src_ref=src, dst_ref=dst, send_sem=ssem, recv_sem=rsem,
                device_id=dev, device_id_type=MESH)

        def start(self):
            pl.when(self.ok)(lambda: self.c.start())

        def sent(self):
            pl.when(self.ok)(lambda: self.c.wait_send())

        def got(self):
            pl.when(self.inc)(lambda: self.c.wait_recv())

    count = [0]

    def msg(d, src, dst):
        i = count[0]
        count[0] += 1
        return Msg(d, src, dst, send.at[i], recv.at[i])

    size = zdim // PARTS
    am, bm = [], []
    for p in range(PARTS):
        zs = pl.ds(p * size, size)
        am.append([
            msg("f", S.at[pl.ds(3, 2), 1, zs], hb_s.at[:, zs]),
            msg("b", S.at[0, 0, zs], ha_xx.at[zs]),
            msg("u", S.at[pl.ds(4, 2), :, zs], hd_s.at[:, :, zs]),
            msg("d", S.at[1, :, zs], hu_yy.at[:, zs]),
        ])
        bm.append([
            msg("f", V.at[2, 1, zs], hb_vx.at[zs]),
            msg("b", V.at[pl.ds(0, 2), 0, zs], ha_v.at[:, zs]),
            msg("u", V.at[0, :, zs], hd_vy.at[:, zs]),
            msg("d", V.at[pl.ds(1, 2), :, zs], hu_v.at[:, :, zs]),
        ])
    csm = [msg("u", csu, hd_cs), msg("d", csd, hu_cs)]
    xsm = [msg("f", xsf, hb_xs), msg("b", xsb, ha_xs)]

    def xm(slot):
        return [
            Msg("f", xf.at[slot], hb_x.at[slot], xsend.at[0, slot], xrecv.at[0, slot]),
            Msg("b", xb.at[slot], ha_x.at[slot], xsend.at[1, slot], xrecv.at[1, slot]),
        ]

    def cm(slot):
        return [
            Msg("u", cu.at[slot], hd_c.at[slot], csend.at[0, slot], crecv.at[0, slot]),
            Msg("d", cd.at[slot], hu_c.at[slot], csend.at[1, slot], crecv.at[1, slot]),
        ]

    def lm(slot):
        return Msg("b", ls.at[slot], lr.at[slot], lsend.at[slot], lrecv.at[slot])

    lane = lax.broadcasted_iota(jnp.int32, (size, 128), 1)
    zrow = lax.broadcasted_iota(jnp.int32, (size, 128), 0)
    lane24 = lax.broadcasted_iota(jnp.int32, (24, 128), 1)
    lane8 = lax.broadcasted_iota(jnp.int32, (8, 128), 1)

    def ym(p, halo):
        return pltpu.roll(jnp.where(lane == 127, halo, p), 1, 1)

    def yp(p, halo):
        return pltpu.roll(jnp.where(lane == 0, halo, p), 127, 1)

    def zm(ref, c, x, z):
        if z == 0:
            return jnp.where(zrow == 0, 0.0, pltpu.roll(ref[c, x, 0:size, :], 1, 0))
        return pltpu.roll(ref[c, x, z - 8:z + size, :], 1, 0)[8:]

    def zp(ref, c, x, z):
        if z + size == zdim:
            return jnp.where(zrow == size - 1, 0.0, pltpu.roll(ref[c, x, z:zdim, :], size - 1, 0))
        return pltpu.roll(ref[c, x, z:z + size + 8, :], size + 7, 0)[:size]

    def rm(a):
        return pltpu.roll(a, 1, 0)

    def rp(a):
        return pltpu.roll(a, a.shape[0] - 1, 0)

    def cmn(a):
        return pltpu.roll(a, 1, 1)

    def cpl(a):
        return pltpu.roll(a, a.shape[1] - 1, 1)

    half = own // 2

    def fill_x(slot):
        for buf, rows in ((xf, slice(12, 16)), (xb, slice(0, 4))):
            buf[slot, 0:4, 0:own] = H[rows, 0:own]
            buf[slot, 4:8, 0:own] = M[rows, 0:own]
            buf[slot, 0:4, own:own + half] = N[rows, 0:half]
            buf[slot, 4:8, own:own + half] = N[rows, half:own]
        t = jnp.concatenate([V[1, 0, 0:1, :], V[1, 1, 0:1, :]], axis=0)
        xf[slot, 0:2, own + half:own + half + 128] = t
        tops[1:3, 0:128] = t

    def use_x(slot):
        at, left, right = slice(0, own), slice(0, half), slice(half, own)
        n = slice(own, own + half)
        a, b = ha_x, hb_x
        H[16:24, at] = jnp.concatenate([a[slot, 0:4, at], b[slot, 0:4, at]], axis=0)
        M[16:24, at] = jnp.concatenate([a[slot, 4:8, at], b[slot, 4:8, at]], axis=0)
        N[16:24, left] = jnp.concatenate([a[slot, 0:4, n], b[slot, 0:4, n]], axis=0)
        N[16:24, right] = jnp.concatenate([a[slot, 4:8, n], b[slot, 4:8, n]], axis=0)
        t = b[slot, 0:2, own + half:own + half + 128]
        tops[0:1, 0:128] = t[1:2, :]
        tops[3:4, 0:128] = t[0:1, :]

    def fill_c(slot):
        for i, r in enumerate((H, M, N)):
            cu[slot, 24 * i:24 * i + 24, :] = r[:, own - 128:own]
            cd[slot, 24 * i:24 * i + 24, :] = r[:, 0:128]
        cu[slot, 72:80, :] = tops[:, 0:128]
        cd[slot, 72:80, :] = tops[:, 0:128]

    def use_c(slot):
        for i, r in enumerate((H, M, N)):
            at = slice(24 * i, 24 * i + 24)
            r[:, own:lanes] = jnp.where(lane24 < 64, hu_c[slot, at, :], hd_c[slot, at, :])
        tops[:, 128:256] = jnp.where(
            lane8 < 8, hu_c[slot, 72:80, :], pltpu.roll(hd_c[slot, 72:80, :], 16, 1))

    def start_all(ms):
        for m in ms:
            m.start()

    for c in loads[:4]:
        c.wait()
    for p in range(PARTS):
        start_all(am[p])
    for c in loads[4:11]:
        c.wait()
    W[0:16, 0:own] = Wi[...].astype(F32)
    for buf, rows in ((xsf, slice(12, 16)), (xsb, slice(0, 4))):
        buf[0:4, 0:own] = W[rows, 0:own]
        buf[4:8, 0:own] = D[rows, 0:own]
    for q in range(own // 128):
        xsb[q:q + 1, own:own + 128] = W[4:5, 128 * q:128 * q + 128]
    fill_x(0)
    for c in loads[11:]:
        c.wait()

    def bed_x():
        at = slice(0, own)
        W[16:24, at] = jnp.concatenate([ha_xs[0:4, at], hb_xs[0:4, at]], axis=0)
        D[16:24, at] = jnp.concatenate([ha_xs[4:8, at], hb_xs[4:8, at]], axis=0)
        w = W[:, at]
        Fx[:, at] = w * rp(w)
        nextw = jnp.concatenate(
            [ha_xs[q:q + 1, own:own + 128] for q in range(own // 128)], axis=1)
        Fx[16:20, at] = W[16:20, at] * jnp.concatenate([W[17:20, at], nextw], axis=0)
        for i, r in enumerate((W, D, Fx)):
            csu[24 * i:24 * i + 24, :] = r[:, own - 128:own]
            csd[24 * i:24 * i + 24, :] = r[:, 0:128]

    def ocean_setup():
        for i, r in enumerate((W, D, Fx)):
            at = slice(24 * i, 24 * i + 24)
            r[:, own:lanes] = jnp.where(lane24 < 64, hu_cs[at, :], hd_cs[at, :])
        w = W[...]
        d = D[...]
        fx = Fx[...]
        fy = w * cpl(w)
        wt[...] = WAVE_STEP * w
        Dx[...] = d + rp(d)
        Dy[...] = d + cpl(d)
        Bx[...] = VISCOSITY * fx
        By[...] = VISCOSITY * fy
        Ax[...] = fx * (1.0 - VISCOSITY * (rp(fx) + rm(fx) + cpl(fx) + cmn(fx)))
        Ay[...] = fy * (1.0 - VISCOSITY * (rp(fy) + rm(fy) + cpl(fy) + cmn(fy)))

    def mask_flow():
        fx = Fx[...]
        fy = W[...] * cpl(W[...])
        m, n = M[...], N[...]
        mm, nn = fx * m, fy * n
        dm, dn = m - mm, n - nn
        H[...] = H[...] - wt[...] * ((dm - rm(dm)) + (dn - cmn(dn)))
        M[...] = mm
        N[...] = nn

    first24, last24 = lane24 == 0, lane24 == 127

    def tile(r, q):
        q = q % nt
        return r[:, 128 * q:128 * q + 128]

    def from_left(a, left):
        return pltpu.roll(jnp.where(last24, left, a), 1, 1)

    def from_right(a, right):
        return pltpu.roll(jnp.where(first24, right, a), 127, 1)

    def substep(_, carry):
        m0, n0 = tile(M, 0), tile(N, 0)
        ml, nl = tile(M, nt - 1), tile(N, nt - 1)
        m, n = m0, n0

        def height(q, m, n, nl):
            mw, ns = rm(m), from_left(n, nl)
            return tile(H, q) - tile(wt, q) * ((m - mw) + (n - ns)), mw, ns

        h0, mw, ns = height(0, m, n, nl)
        h = h0
        for q in range(nt):
            at = slice(128 * q, 128 * q + 128)
            H[:, at] = h
            if q < nt - 1:
                mr, nr = tile(M, q + 1), tile(N, q + 1)
                hr, mwr, nsr = height(q + 1, mr, nr, n)
            else:
                mr, nr, hr, mwr, nsr = m0, n0, h0, None, None
            he, hn = rp(h), from_right(h, hr)
            M[:, at] = tile(Ax, q) * m + tile(Bx, q) * (
                ((rp(m) + mw) + (from_right(m, mr) + from_left(m, ml)))
                - (tile(Dx, q) + h + he) * (he - h))
            N[:, at] = tile(Ay, q) * n + tile(By, q) * (
                ((rp(n) + rm(n)) + (from_right(n, nr) + ns))
                - (tile(Dy, q) + h + hn) * (hn - h))
            ml, m, n, h, mw, ns = m, mr, nr, hr, mwr, nsr
        return carry

    er = lax.broadcasted_iota(jnp.int32, (128, 128), 0)
    ec = lax.broadcasted_iota(jnp.int32, (128, 128), 1)
    row24 = lax.broadcasted_iota(jnp.int32, (24, 128), 0)

    def spread_dot(a, ones):
        p0 = a.astype(jnp.bfloat16)
        r = a - p0.astype(F32)
        p1 = r.astype(jnp.bfloat16)
        p2 = (r - p1.astype(F32)).astype(jnp.bfloat16)
        e = ones.astype(jnp.bfloat16)
        return jnp.dot(jnp.concatenate([p0, p1, p2], axis=1),
                       jnp.concatenate([e, e, e], axis=0), preferred_element_type=F32)

    def lift():
        t = tops[:, 0:128]
        tiles = [t] + [pltpu.roll(t, 128 - 16 * q, 1) for q in range(1, nt - 1)]
        tiles.append(tops[:, 128:256])
        spread = jnp.where((ec // RATIO) == er, 1.0, 0.0)
        u = spread_dot(jnp.concatenate(tiles, axis=0), spread)
        for q in range(nt):
            r = u[8 * q:8 * q + 8, :]
            e = [jnp.broadcast_to(r[i:i + 1, :], (24, 128)) for i in range(4)]
            full = jnp.where(row24 < 8, e[0], jnp.where(row24 < 16, e[1], jnp.where(row24 < 20, e[2], e[3])))
            at = slice(128 * q, 128 * q + 128)
            H[:, at] = H[:, at] + UPLIFT_GAIN * W[:, at] * full

    def average(slot):
        p = W[0:16, 0:own] * H[0:16, 0:own]
        parts = [p[:, 128 * q:128 * q + 128] for q in range(nt - 1)]
        gather = jnp.where((er // RATIO) == ec, 1.0, 0.0)
        g = spread_dot(jnp.concatenate(parts, axis=0), gather)
        a0, a1 = g[0:8, :], g[8:16, :]
        for q in range(1, nt - 1):
            a0 = a0 + pltpu.roll(g[16 * q:16 * q + 8, :], 16 * q, 1)
            a1 = a1 + pltpu.roll(g[16 * q + 8:16 * q + 16, :], 16 * q, 1)
        scale = -LOAD_GAIN / (RATIO * RATIO)
        ls[slot, 0:1, :] = jnp.sum(a0, axis=0, keepdims=True) * scale
        ls[slot, 1:2, :] = jnp.sum(a1, axis=0, keepdims=True) * scale
        lm(slot).start()

    def apply_load(slot):
        lm(slot).got()
        S[2, 0, 0:1, :] = ls[slot, 1:2, :]
        S[2, 1, 0:1, :] = lr[slot, 0:1, :]

    def motion_part(z):
        zs = slice(z, z + size)
        for x in range(2):
            sb = SOLID_STEP * Bu[x, zs]
            xx, yy, zz, xz, xy, yz = (S[c, x, zs] for c in range(6))
            xx_a = S[0, 1, zs] if x == 0 else ha_xx[zs]
            xz_b = hb_s[0, zs] if x == 0 else S[3, 0, zs]
            xy_b = hb_s[1, zs] if x == 0 else S[4, 0, zs]
            V[2, x, zs] = V[2, x, zs] + sb * (
                (xx_a - xx) + (xy - ym(xy, hd_s[0, x, zs])) + (xz - zm(S, 3, x, z)))
            V[0, x, zs] = V[0, x, zs] + sb * (
                (xy - xy_b) + (yp(yy, hu_yy[x, zs]) - yy) + (yz - zm(S, 5, x, z)))
            V[1, x, zs] = V[1, x, zs] + sb * (
                (xz - xz_b) + (yz - ym(yz, hd_s[1, x, zs])) + (zp(S, 2, x, z) - zz))

    def stress_part(z):
        zs = slice(z, z + size)
        for x in range(2):
            vy, vz, vx = V[0, x, zs], V[1, x, zs], V[2, x, zs]
            vx_b = hb_vx[zs] if x == 0 else V[2, 0, zs]
            vy_a = V[0, 1, zs] if x == 0 else ha_v[0, zs]
            vz_a = V[1, 1, zs] if x == 0 else ha_v[1, zs]
            ex = vx - vx_b
            ey = vy - ym(vy, hd_vy[x, zs])
            ez = vz - zm(V, 1, x, z)
            l, g = SOLID_STEP * L1[x, zs], SOLID_STEP * L2[x, zs]
            tr = l * (ex + ey + ez)
            g2 = 2.0 * g
            S[0, x, zs] = S[0, x, zs] + (tr + g2 * ex)
            S[1, x, zs] = S[1, x, zs] + (tr + g2 * ey)
            S[2, x, zs] = S[2, x, zs] + (tr + g2 * ez)
            S[3, x, zs] = S[3, x, zs] + g * ((zp(V, 2, x, z) - vx) + (vz_a - vz))
            S[4, x, zs] = S[4, x, zs] + g * ((yp(vx, hu_v[1, x, zs]) - vx) + (vy_a - vy))
            S[5, x, zs] = S[5, x, zs] + g * ((zp(V, 0, x, z) - vy) + (yp(vz, hu_v[0, x, zs]) - vz))

    def step(k, carry):
        slot = lax.rem(k, 2)
        nslot = lax.rem(k + 1, 2)

        xms = xm(slot)
        cms = cm(slot)
        for ms in am:
            for m in ms:
                m.sent()
        start_all(xms)
        pl.when(k == 0)(lambda: start_all(xsm))

        for p in range(PARTS):
            for m in am[p]:
                m.got()
            if p == 0:
                @pl.when(k > 0)
                def _():
                    apply_load(nslot)

            motion_part(p * size)
            start_all(bm[p])

        for m in xms:
            m.got()
        use_x(slot)

        @pl.when(k == 0)
        def _():
            for m in xsm:
                m.got()
            bed_x()
            start_all(csm)

        fill_c(slot)
        start_all(cms)
        for m in cms:
            m.got()
        use_c(slot)

        @pl.when(k == 0)
        def _():
            for m in csm:
                m.got()
            ocean_setup()
            mask_flow()

        lift()
        lax.fori_loop(0, NSUB, substep, 0)
        last = k == STEPS - 1
        pl.when(last)(lambda: average(slot))

        @pl.when(k < STEPS - 1)
        def _():
            fill_x(nslot)

        for p in range(PARTS):
            for m in bm[p]:
                m.got()
            stress_part(p * size)

            @pl.when(k < STEPS - 1)
            def _():
                start_all(am[p])

        pl.when(jnp.logical_not(last))(lambda: average(slot))
        for ms in bm:
            for m in ms:
                m.sent()
        for m in xms + cms:
            m.sent()
        lm(slot).sent()
        return carry

    lax.fori_loop(0, STEPS, step, 0)
    for m in xsm + csm:
        m.sent()
    apply_load((STEPS - 1) % 2)


def write_out(V, S, H, M, N, o_motion, o_stress, o_surf, o_mom, sem):
    rows, own = o_surf.shape
    at = (pl.ds(0, rows), pl.ds(0, own))
    outs = [
        pltpu.make_async_copy(a, b, sem.at[i])
        for i, (a, b) in enumerate([
            (S.at[pl.ds(0, 3)], o_stress.at[pl.ds(0, 3)]),
            (V.at[pl.ds(0, 2)], o_motion.at[pl.ds(1, 2)]), (V.at[2], o_motion.at[0]),
            (S.at[4], o_stress.at[3]), (S.at[3], o_stress.at[4]), (S.at[5], o_stress.at[5]),
            (H.at[at], o_surf), (M.at[at], o_mom.at[0]), (N.at[at], o_mom.at[1]),
        ])
    ]
    for c in outs:
        c.start()
    for c in outs:
        c.wait()


def body(nx, ny, motion, stress, buoyancy, lame_first, lame_shear, surface, momentum, bathymetry, wet_mask):
    plane = motion.shape[2:]
    two = motion.shape[1:]
    ext = (24, surface.shape[1] + 128)

    def v(*shape):
        return pltpu.VMEM(shape, F32)

    scratch = [v(*two)] * 3 + [pltpu.VMEM(wet_mask.shape, jnp.int32)] + [v(*ext)] * 10
    scratch += [v(2, *plane), v(*plane), v(2, *two), v(*two)]
    scratch += [v(*plane), v(2, *plane), v(*two), v(2, *two)]
    scratch += [v(2, 80, 128)] * 4 + [v(72, 128)] * 4
    wide = surface.shape[1]
    scratch += [v(2, 8, wide + wide // 2 + 128)] * 4 + [v(8, wide + 128)] * 4
    scratch += [v(2, 8, 128), v(2, 8, 128), v(8, 256)]
    dma = pltpu.SemaphoreType.DMA
    scratch += [dma((14,)), dma((8 * PARTS + 4,)), dma((8 * PARTS + 4,)), dma((2, 2)), dma((2, 2)), dma((2, 2)), dma((2, 2)), dma((2,)), dma((2,))]
    state = [motion.shape, stress.shape, ext, ext, ext]
    hbm = pl.BlockSpec(memory_space=pltpu.HBM)
    held = pl.pallas_call(
        functools.partial(kernel, nx, ny),
        out_shape=[pltpu.VMEM(shape, F32) for shape in state],
        in_specs=[hbm] * 9,
        out_specs=[pl.BlockSpec(memory_space=pltpu.VMEM)] * 5,
        scratch_shapes=scratch,
        compiler_params=pltpu.CompilerParams(
            collective_id=0, has_side_effects=True, vmem_limit_bytes=56 * 1024 * 1024
        ),
        name="coupled",
    )(motion, stress, buoyancy, lame_first, lame_shear, surface, momentum, bathymetry, wet_mask)
    return pl.pallas_call(
        write_out,
        out_shape=[
            jax.ShapeDtypeStruct(a.shape, F32) for a in (motion, stress, surface, momentum)
        ],
        in_specs=[pl.BlockSpec(memory_space=pl.ANY)] * 5,
        out_specs=[pl.BlockSpec(memory_space=pl.ANY)] * 4,
        scratch_shapes=[dma((9,))],
        compiler_params=pltpu.CompilerParams(vmem_limit_bytes=1024 * 1024),
        name="write_out",
    )(*held)


def solution(mesh):
    return jax.shard_map(
        functools.partial(body, mesh.shape["gx"], mesh.shape["gy"]),
        mesh=mesh,
        in_specs=(
            P(None, "gx", None, "gy"),
            P(None, "gx", None, "gy"),
            P("gx", None, "gy"),
            P("gx", None, "gy"),
            P("gx", None, "gy"),
            P("gx", "gy"),
            P(None, "gx", "gy"),
            P("gx", "gy"),
            P("gx", "gy"),
        ),
        out_specs=(
            P(None, "gx", None, "gy"),
            P(None, "gx", None, "gy"),
            P("gx", "gy"),
            P(None, "gx", "gy"),
        ),
        check_vma=False,
    )
```

```python
import functools

import jax
import jax.numpy as jnp
from jax import lax
from jax.experimental import pallas as pl
from jax.experimental.pallas import tpu as pltpu
from jax.sharding import PartitionSpec as P

RATIO = 8
STEPS = 4
NSUB = 4
PARTS = 2
SOLID_STEP = 0.2
WAVE_STEP = 0.1
VISCOSITY = 0.05
UPLIFT_GAIN = 0.25
LOAD_GAIN = 8.0

MESH = pl.DeviceIdType.MESH
F32 = jnp.float32


def kernel(
    nx, ny,
    motion, stress, buoy, lame1, lame2, surf, mom, bath, wetm,
    V, S, H, M, N,
    Bu, L1, L2, Wi, W, D, wt, Dx, Dy, Ax, Bx, Ay, By, Fx,
    hb_s, ha_xx, hd_s, hu_yy,
    hb_vx, ha_v, hd_vy, hu_v,
    cu, cd, hd_c, hu_c, csu, csd, hd_cs, hu_cs,
    xf, xb, hb_x, ha_x, xsf, xsb, hb_xs, ha_xs,
    ls, lr, tops,
    in_sem, send, recv, csend, crecv, xsend, xrecv, lsend, lrecv,
):
    gx = lax.axis_index("gx")
    gy = lax.axis_index("gy")
    has_b, has_a, has_d, has_u = gx > 0, gx < nx - 1, gy > 0, gy < ny - 1
    ahead = (jnp.minimum(gx + 1, nx - 1), gy)
    behind = (jnp.maximum(gx - 1, 0), gy)
    up = (gx, jnp.minimum(gy + 1, ny - 1))
    down = (gx, jnp.maximum(gy - 1, 0))
    dirs = {
        "f": (ahead, has_a, has_b),
        "b": (behind, has_b, has_a),
        "u": (up, has_u, has_d),
        "d": (down, has_d, has_u),
    }
    zdim = S.shape[2]
    lanes = H.shape[1]
    own = surf.shape[1]
    nt = lanes // 128

    loads = [
        pltpu.make_async_copy(a, b, in_sem.at[i])
        for i, (a, b) in enumerate([
            (stress.at[pl.ds(0, 3)], S.at[pl.ds(0, 3)]), (stress.at[3], S.at[4]),
            (stress.at[4], S.at[3]), (stress.at[5], S.at[5]),
            (wetm, Wi),
            (bath, D.at[pl.ds(0, 16), pl.ds(0, own)]),
            (surf, H.at[pl.ds(0, 16), pl.ds(0, own)]),
            (mom.at[0], M.at[pl.ds(0, 16), pl.ds(0, own)]),
            (mom.at[1], N.at[pl.ds(0, 16), pl.ds(0, own)]),
            (motion.at[pl.ds(1, 2)], V.at[pl.ds(0, 2)]), (motion.at[0], V.at[2]),
            (buoy, Bu), (lame1, L1), (lame2, L2),
        ])
    ]
    for c in loads:
        c.start()

    def zero_when_absent(flag, refs):
        @pl.when(jnp.logical_not(flag))
        def _():
            for r in refs:
                r[...] = jnp.zeros(r.shape, F32)

    zero_when_absent(has_b, [hb_s, hb_vx, hb_x, hb_xs])
    zero_when_absent(has_a, [ha_xx, ha_v, ha_x, ha_xs, lr])
    zero_when_absent(has_d, [hd_s, hd_vy, hd_c, hd_cs])
    zero_when_absent(has_u, [hu_yy, hu_v, hu_c, hu_cs])
    for r in (xf, xb, xsf, xsb, ls, tops):
        r[...] = jnp.zeros(r.shape, F32)

    barrier = pltpu.get_barrier_semaphore()
    for d in "fbud":
        dev, ok, _ = dirs[d]

        @pl.when(ok)
        def _():
            pl.semaphore_signal(barrier, inc=1, device_id=dev, device_id_type=MESH)

    pl.semaphore_wait(barrier, sum(f.astype(jnp.int32) for f in (has_b, has_a, has_d, has_u)))

    class Msg:
        def __init__(self, d, src, dst, ssem, rsem):
            dev, self.ok, self.inc = dirs[d]
            self.c = pltpu.make_async_remote_copy(
                src_ref=src, dst_ref=dst, send_sem=ssem, recv_sem=rsem,
                device_id=dev, device_id_type=MESH)

        def start(self):
            pl.when(self.ok)(lambda: self.c.start())

        def sent(self):
            pl.when(self.ok)(lambda: self.c.wait_send())

        def got(self):
            pl.when(self.inc)(lambda: self.c.wait_recv())

    count = [0]

    def msg(d, src, dst):
        i = count[0]
        count[0] += 1
        return Msg(d, src, dst, send.at[i], recv.at[i])

    size = zdim // PARTS
    am, bm = [], []
    for p in range(PARTS):
        zs = pl.ds(p * size, size)
        am.append([
            msg("f", S.at[pl.ds(3, 2), 1, zs], hb_s.at[:, zs]),
            msg("b", S.at[0, 0, zs], ha_xx.at[zs]),
            msg("u", S.at[pl.ds(4, 2), :, zs], hd_s.at[:, :, zs]),
            msg("d", S.at[1, :, zs], hu_yy.at[:, zs]),
        ])
        bm.append([
            msg("f", V.at[2, 1, zs], hb_vx.at[zs]),
            msg("b", V.at[pl.ds(0, 2), 0, zs], ha_v.at[:, zs]),
            msg("u", V.at[0, :, zs], hd_vy.at[:, zs]),
            msg("d", V.at[pl.ds(1, 2), :, zs], hu_v.at[:, :, zs]),
        ])
    csm = [msg("u", csu, hd_cs), msg("d", csd, hu_cs)]
    xsm = [msg("f", xsf, hb_xs), msg("b", xsb, ha_xs)]

    def xm(slot):
        return [
            Msg("f", xf.at[slot], hb_x.at[slot], xsend.at[0, slot], xrecv.at[0, slot]),
            Msg("b", xb.at[slot], ha_x.at[slot], xsend.at[1, slot], xrecv.at[1, slot]),
        ]

    def cm(slot):
        return [
            Msg("u", cu.at[slot], hd_c.at[slot], csend.at[0, slot], crecv.at[0, slot]),
            Msg("d", cd.at[slot], hu_c.at[slot], csend.at[1, slot], crecv.at[1, slot]),
        ]

    def lm(slot):
        return Msg("b", ls.at[slot], lr.at[slot], lsend.at[slot], lrecv.at[slot])

    lane = lax.broadcasted_iota(jnp.int32, (size, 128), 1)
    zrow = lax.broadcasted_iota(jnp.int32, (size, 128), 0)
    lane24 = lax.broadcasted_iota(jnp.int32, (24, 128), 1)
    lane8 = lax.broadcasted_iota(jnp.int32, (8, 128), 1)

    def ym(p, halo):
        return pltpu.roll(jnp.where(lane == 127, halo, p), 1, 1)

    def yp(p, halo):
        return pltpu.roll(jnp.where(lane == 0, halo, p), 127, 1)

    def zm(ref, c, x, z):
        if z == 0:
            return jnp.where(zrow == 0, 0.0, pltpu.roll(ref[c, x, 0:size, :], 1, 0))
        return pltpu.roll(ref[c, x, z - 8:z + size, :], 1, 0)[8:]

    def zp(ref, c, x, z):
        if z + size == zdim:
            return jnp.where(zrow == size - 1, 0.0, pltpu.roll(ref[c, x, z:zdim, :], size - 1, 0))
        return pltpu.roll(ref[c, x, z:z + size + 8, :], size + 7, 0)[:size]

    def rm(a):
        return pltpu.roll(a, 1, 0)

    def rp(a):
        return pltpu.roll(a, a.shape[0] - 1, 0)

    def cmn(a):
        return pltpu.roll(a, 1, 1)

    def cpl(a):
        return pltpu.roll(a, a.shape[1] - 1, 1)

    half = own // 2

    def fill_x(slot):
        for buf, rows in ((xf, slice(12, 16)), (xb, slice(0, 4))):
            buf[slot, 0:4, 0:own] = H[rows, 0:own]
            buf[slot, 4:8, 0:own] = M[rows, 0:own]
            buf[slot, 0:4, own:own + half] = N[rows, 0:half]
            buf[slot, 4:8, own:own + half] = N[rows, half:own]
        t = jnp.concatenate([V[1, 0, 0:1, :], V[1, 1, 0:1, :]], axis=0)
        xf[slot, 0:2, own + half:own + half + 128] = t
        tops[1:3, 0:128] = t

    def use_x(slot):
        at, left, right = slice(0, own), slice(0, half), slice(half, own)
        n = slice(own, own + half)
        a, b = ha_x, hb_x
        H[16:24, at] = jnp.concatenate([a[slot, 0:4, at], b[slot, 0:4, at]], axis=0)
        M[16:24, at] = jnp.concatenate([a[slot, 4:8, at], b[slot, 4:8, at]], axis=0)
        N[16:24, left] = jnp.concatenate([a[slot, 0:4, n], b[slot, 0:4, n]], axis=0)
        N[16:24, right] = jnp.concatenate([a[slot, 4:8, n], b[slot, 4:8, n]], axis=0)
        t = b[slot, 0:2, own + half:own + half + 128]
        tops[0:1, 0:128] = t[1:2, :]
        tops[3:4, 0:128] = t[0:1, :]

    def fill_c(slot):
        for i, r in enumerate((H, M, N)):
            cu[slot, 24 * i:24 * i + 24, :] = r[:, own - 128:own]
            cd[slot, 24 * i:24 * i + 24, :] = r[:, 0:128]
        cu[slot, 72:80, :] = tops[:, 0:128]
        cd[slot, 72:80, :] = tops[:, 0:128]

    def use_c(slot):
        for i, r in enumerate((H, M, N)):
            at = slice(24 * i, 24 * i + 24)
            r[:, own:lanes] = jnp.where(lane24 < 64, hu_c[slot, at, :], hd_c[slot, at, :])
        tops[:, 128:256] = jnp.where(
            lane8 < 8, hu_c[slot, 72:80, :], pltpu.roll(hd_c[slot, 72:80, :], 16, 1))

    def start_all(ms):
        for m in ms:
            m.start()

    for c in loads[:4]:
        c.wait()
    for p in range(PARTS):
        start_all(am[p])
    for c in loads[4:11]:
        c.wait()
    W[0:16, 0:own] = Wi[...].astype(F32)
    for buf, rows in ((xsf, slice(12, 16)), (xsb, slice(0, 4))):
        buf[0:4, 0:own] = W[rows, 0:own]
        buf[4:8, 0:own] = D[rows, 0:own]
    for q in range(own // 128):
        xsb[q:q + 1, own:own + 128] = W[4:5, 128 * q:128 * q + 128]
    fill_x(0)
    start_all(xm(0))
    start_all(xsm)
    for c in loads[11:]:
        c.wait()

    def bed_x():
        at = slice(0, own)
        W[16:24, at] = jnp.concatenate([ha_xs[0:4, at], hb_xs[0:4, at]], axis=0)
        D[16:24, at] = jnp.concatenate([ha_xs[4:8, at], hb_xs[4:8, at]], axis=0)
        w = W[:, at]
        Fx[:, at] = w * rp(w)
        nextw = jnp.concatenate(
            [ha_xs[q:q + 1, own:own + 128] for q in range(own // 128)], axis=1)
        Fx[16:20, at] = W[16:20, at] * jnp.concatenate([W[17:20, at], nextw], axis=0)
        for i, r in enumerate((W, D, Fx)):
            csu[24 * i:24 * i + 24, :] = r[:, own - 128:own]
            csd[24 * i:24 * i + 24, :] = r[:, 0:128]

    def ocean_setup():
        for i, r in enumerate((W, D, Fx)):
            at = slice(24 * i, 24 * i + 24)
            r[:, own:lanes] = jnp.where(lane24 < 64, hu_cs[at, :], hd_cs[at, :])
        w = W[...]
        d = D[...]
        fx = Fx[...]
        fy = w * cpl(w)
        wt[...] = WAVE_STEP * w
        Dx[...] = d + rp(d)
        Dy[...] = d + cpl(d)
        Bx[...] = VISCOSITY * fx
        By[...] = VISCOSITY * fy
        Ax[...] = fx * (1.0 - VISCOSITY * (rp(fx) + rm(fx) + cpl(fx) + cmn(fx)))
        Ay[...] = fy * (1.0 - VISCOSITY * (rp(fy) + rm(fy) + cpl(fy) + cmn(fy)))

    def mask_flow():
        fx = Fx[...]
        fy = W[...] * cpl(W[...])
        m, n = M[...], N[...]
        mm, nn = fx * m, fy * n
        dm, dn = m - mm, n - nn
        H[...] = H[...] - wt[...] * ((dm - rm(dm)) + (dn - cmn(dn)))
        M[...] = mm
        N[...] = nn

    first24, last24 = lane24 == 0, lane24 == 127

    def tile(r, q):
        q = q % nt
        return r[:, 128 * q:128 * q + 128]

    def from_left(a, left):
        return pltpu.roll(jnp.where(last24, left, a), 1, 1)

    def from_right(a, right):
        return pltpu.roll(jnp.where(first24, right, a), 127, 1)

    def substep(_, carry):
        m0, n0 = tile(M, 0), tile(N, 0)
        ml, nl = tile(M, nt - 1), tile(N, nt - 1)
        m, n = m0, n0

        def height(q, m, n, nl):
            mw, ns = rm(m), from_left(n, nl)
            return tile(H, q) - tile(wt, q) * ((m - mw) + (n - ns)), mw, ns

        h0, mw, ns = height(0, m, n, nl)
        h = h0
        for q in range(nt):
            at = slice(128 * q, 128 * q + 128)
            H[:, at] = h
            if q < nt - 1:
                mr, nr = tile(M, q + 1), tile(N, q + 1)
                hr, mwr, nsr = height(q + 1, mr, nr, n)
            else:
                mr, nr, hr, mwr, nsr = m0, n0, h0, None, None
            he, hn = rp(h), from_right(h, hr)
            M[:, at] = tile(Ax, q) * m + tile(Bx, q) * (
                ((rp(m) + mw) + (from_right(m, mr) + from_left(m, ml)))
                - (tile(Dx, q) + h + he) * (he - h))
            N[:, at] = tile(Ay, q) * n + tile(By, q) * (
                ((rp(n) + rm(n)) + (from_right(n, nr) + ns))
                - (tile(Dy, q) + h + hn) * (hn - h))
            ml, m, n, h, mw, ns = m, mr, nr, hr, mwr, nsr
        return carry

    er = lax.broadcasted_iota(jnp.int32, (128, 128), 0)
    ec = lax.broadcasted_iota(jnp.int32, (128, 128), 1)
    row24 = lax.broadcasted_iota(jnp.int32, (24, 128), 0)

    def spread_dot(a, ones):
        p0 = a.astype(jnp.bfloat16)
        r = a - p0.astype(F32)
        p1 = r.astype(jnp.bfloat16)
        p2 = (r - p1.astype(F32)).astype(jnp.bfloat16)
        e = ones.astype(jnp.bfloat16)
        return jnp.dot(jnp.concatenate([p0, p1, p2], axis=1),
                       jnp.concatenate([e, e, e], axis=0), preferred_element_type=F32)

    def lift():
        t = tops[:, 0:128]
        tiles = [t] + [pltpu.roll(t, 128 - 16 * q, 1) for q in range(1, nt - 1)]
        tiles.append(tops[:, 128:256])
        spread = jnp.where((ec // RATIO) == er, 1.0, 0.0)
        u = spread_dot(jnp.concatenate(tiles, axis=0), spread)
        for q in range(nt):
            r = u[8 * q:8 * q + 8, :]
            e = [jnp.broadcast_to(r[i:i + 1, :], (24, 128)) for i in range(4)]
            full = jnp.where(row24 < 8, e[0], jnp.where(row24 < 16, e[1], jnp.where(row24 < 20, e[2], e[3])))
            at = slice(128 * q, 128 * q + 128)
            H[:, at] = H[:, at] + UPLIFT_GAIN * W[:, at] * full

    def average(slot):
        p = W[0:16, 0:own] * H[0:16, 0:own]
        parts = [p[:, 128 * q:128 * q + 128] for q in range(nt - 1)]
        gather = jnp.where((er // RATIO) == ec, 1.0, 0.0)
        g = spread_dot(jnp.concatenate(parts, axis=0), gather)
        a0, a1 = g[0:8, :], g[8:16, :]
        for q in range(1, nt - 1):
            a0 = a0 + pltpu.roll(g[16 * q:16 * q + 8, :], 16 * q, 1)
            a1 = a1 + pltpu.roll(g[16 * q + 8:16 * q + 16, :], 16 * q, 1)
        scale = -LOAD_GAIN / (RATIO * RATIO)
        ls[slot, 0:1, :] = jnp.sum(a0, axis=0, keepdims=True) * scale
        ls[slot, 1:2, :] = jnp.sum(a1, axis=0, keepdims=True) * scale
        lm(slot).start()

    def apply_load(slot):
        lm(slot).got()
        S[2, 0, 0:1, :] = ls[slot, 1:2, :]
        S[2, 1, 0:1, :] = lr[slot, 0:1, :]

    def motion_part(z):
        zs = slice(z, z + size)
        for x in range(2):
            sb = SOLID_STEP * Bu[x, zs]
            xx, yy, zz, xz, xy, yz = (S[c, x, zs] for c in range(6))
            xx_a = S[0, 1, zs] if x == 0 else ha_xx[zs]
            xz_b = hb_s[0, zs] if x == 0 else S[3, 0, zs]
            xy_b = hb_s[1, zs] if x == 0 else S[4, 0, zs]
            V[2, x, zs] = V[2, x, zs] + sb * (
                (xx_a - xx) + (xy - ym(xy, hd_s[0, x, zs])) + (xz - zm(S, 3, x, z)))
            V[0, x, zs] = V[0, x, zs] + sb * (
                (xy - xy_b) + (yp(yy, hu_yy[x, zs]) - yy) + (yz - zm(S, 5, x, z)))
            V[1, x, zs] = V[1, x, zs] + sb * (
                (xz - xz_b) + (yz - ym(yz, hd_s[1, x, zs])) + (zp(S, 2, x, z) - zz))

    def stress_part(z):
        zs = slice(z, z + size)
        for x in range(2):
            vy, vz, vx = V[0, x, zs], V[1, x, zs], V[2, x, zs]
            vx_b = hb_vx[zs] if x == 0 else V[2, 0, zs]
            vy_a = V[0, 1, zs] if x == 0 else ha_v[0, zs]
            vz_a = V[1, 1, zs] if x == 0 else ha_v[1, zs]
            ex = vx - vx_b
            ey = vy - ym(vy, hd_vy[x, zs])
            ez = vz - zm(V, 1, x, z)
            l, g = SOLID_STEP * L1[x, zs], SOLID_STEP * L2[x, zs]
            tr = l * (ex + ey + ez)
            g2 = 2.0 * g
            S[0, x, zs] = S[0, x, zs] + (tr + g2 * ex)
            S[1, x, zs] = S[1, x, zs] + (tr + g2 * ey)
            S[2, x, zs] = S[2, x, zs] + (tr + g2 * ez)
            S[3, x, zs] = S[3, x, zs] + g * ((zp(V, 2, x, z) - vx) + (vz_a - vz))
            S[4, x, zs] = S[4, x, zs] + g * ((yp(vx, hu_v[1, x, zs]) - vx) + (vy_a - vy))
            S[5, x, zs] = S[5, x, zs] + g * ((zp(V, 0, x, z) - vy) + (yp(vz, hu_v[0, x, zs]) - vz))

    def waves(k, slot):
        for m in xm(slot):
            m.got()
        use_x(slot)

        @pl.when(k == 0)
        def _():
            for m in xsm:
                m.got()
            bed_x()
            start_all(csm)

        fill_c(slot)
        start_all(cm(slot))
        for m in cm(slot):
            m.got()
        use_c(slot)

        @pl.when(k == 0)
        def _():
            for m in csm:
                m.got()
            ocean_setup()
            mask_flow()

        lift()
        lax.fori_loop(0, NSUB, substep, 0)
        average(slot)

    def step(k, carry):
        slot = lax.rem(k, 2)
        nslot = lax.rem(k + 1, 2)

        pl.when(k > 0)(lambda: waves(k, slot))
        for p in range(PARTS):
            for m in am[p]:
                m.got()
            if p == 0:
                @pl.when(k > 0)
                def _():
                    apply_load(nslot)

            motion_part(p * size)
            start_all(bm[p])

        pl.when(k == 0)(lambda: waves(k, slot))

        @pl.when(k < STEPS - 1)
        def _():
            fill_x(nslot)

        for ms in bm:
            for m in ms:
                m.sent()

        @pl.when(k < STEPS - 1)
        def _():
            start_all(xm(nslot))

        for p in range(PARTS):
            for m in bm[p]:
                m.got()
            for m in am[p]:
                m.sent()
            stress_part(p * size)

            @pl.when(k < STEPS - 1)
            def _():
                start_all(am[p])

        for m in xm(slot) + cm(slot):
            m.sent()
        lm(slot).sent()
        return carry

    lax.fori_loop(0, STEPS, step, 0)
    for m in xsm + csm:
        m.sent()
    apply_load((STEPS - 1) % 2)


def write_out(V, S, H, M, N, o_motion, o_stress, o_surf, o_mom, sem):
    rows, own = o_surf.shape
    at = (pl.ds(0, rows), pl.ds(0, own))
    outs = [
        pltpu.make_async_copy(a, b, sem.at[i])
        for i, (a, b) in enumerate([
            (S.at[pl.ds(0, 3)], o_stress.at[pl.ds(0, 3)]),
            (V.at[pl.ds(0, 2)], o_motion.at[pl.ds(1, 2)]), (V.at[2], o_motion.at[0]),
            (S.at[4], o_stress.at[3]), (S.at[3], o_stress.at[4]), (S.at[5], o_stress.at[5]),
            (H.at[at], o_surf), (M.at[at], o_mom.at[0]), (N.at[at], o_mom.at[1]),
        ])
    ]
    for c in outs:
        c.start()
    for c in outs:
        c.wait()


def body(nx, ny, motion, stress, buoyancy, lame_first, lame_shear, surface, momentum, bathymetry, wet_mask):
    plane = motion.shape[2:]
    two = motion.shape[1:]
    ext = (24, surface.shape[1] + 128)

    def v(*shape):
        return pltpu.VMEM(shape, F32)

    scratch = [v(*two)] * 3 + [pltpu.VMEM(wet_mask.shape, jnp.int32)] + [v(*ext)] * 10
    scratch += [v(2, *plane), v(*plane), v(2, *two), v(*two)]
    scratch += [v(*plane), v(2, *plane), v(*two), v(2, *two)]
    scratch += [v(2, 80, 128)] * 4 + [v(72, 128)] * 4
    wide = surface.shape[1]
    scratch += [v(2, 8, wide + wide // 2 + 128)] * 4 + [v(8, wide + 128)] * 4
    scratch += [v(2, 8, 128), v(2, 8, 128), v(8, 256)]
    dma = pltpu.SemaphoreType.DMA
    scratch += [dma((14,)), dma((8 * PARTS + 4,)), dma((8 * PARTS + 4,)), dma((2, 2)), dma((2, 2)), dma((2, 2)), dma((2, 2)), dma((2,)), dma((2,))]
    state = [motion.shape, stress.shape, ext, ext, ext]
    hbm = pl.BlockSpec(memory_space=pltpu.HBM)
    held = pl.pallas_call(
        functools.partial(kernel, nx, ny),
        out_shape=[pltpu.VMEM(shape, F32) for shape in state],
        in_specs=[hbm] * 9,
        out_specs=[pl.BlockSpec(memory_space=pltpu.VMEM)] * 5,
        scratch_shapes=scratch,
        compiler_params=pltpu.CompilerParams(
            collective_id=0, has_side_effects=True, vmem_limit_bytes=56 * 1024 * 1024
        ),
        name="coupled",
    )(motion, stress, buoyancy, lame_first, lame_shear, surface, momentum, bathymetry, wet_mask)
    return pl.pallas_call(
        write_out,
        out_shape=[
            jax.ShapeDtypeStruct(a.shape, F32) for a in (motion, stress, surface, momentum)
        ],
        in_specs=[pl.BlockSpec(memory_space=pl.ANY)] * 5,
        out_specs=[pl.BlockSpec(memory_space=pl.ANY)] * 4,
        scratch_shapes=[dma((9,))],
        compiler_params=pltpu.CompilerParams(vmem_limit_bytes=1024 * 1024),
        name="write_out",
    )(*held)


def solution(mesh):
    return jax.shard_map(
        functools.partial(body, mesh.shape["gx"], mesh.shape["gy"]),
        mesh=mesh,
        in_specs=(
            P(None, "gx", None, "gy"),
            P(None, "gx", None, "gy"),
            P("gx", None, "gy"),
            P("gx", None, "gy"),
            P("gx", None, "gy"),
            P("gx", "gy"),
            P(None, "gx", "gy"),
            P("gx", "gy"),
            P("gx", "gy"),
        ),
        out_specs=(
            P(None, "gx", None, "gy"),
            P(None, "gx", None, "gy"),
            P("gx", "gy"),
            P(None, "gx", "gy"),
        ),
        check_vma=False,
    )
```
